32 devices in a mesh: img: 4 (over x, core), row: 8 (over z, y).
Axes of the slice: x: 2, y: 2, z: 4, core: 2. Of those that a mesh axis runs over, the one named last changes fastest.
Arguments:
- feats2: bfloat16 [32, 64, 16, 256], P('img', 'row'), may hold values from -6 to 6
- feats3: bfloat16 [32, 32, 8, 512], P(('img', 'row')), may hold values from -6 to 6
- match2: int32 [32, 3, 64, 16], P('img', None, 'row'), may hold values 0 or 1
- target2: float32 [32, 12, 64, 16], P('img', None, 'row'), may hold values from -6 to 6
- match3: int32 [32, 3, 32, 8], P(('img', 'row')), may hold values 0 or 1
- target3: float32 [32, 12, 32, 8], P(('img', 'row')), may hold values from -6 to 6
- positives: int32 [], replicated, may hold values from 6144 to 10239
- step_count: int32 [], replicated, may hold values from 1 to 20
- lat2_w: float32 [256, 256], replicated, may hold values from -0.375 to 0.375
- lat2_m: float32 [256, 256], replicated, may hold values from -0.0007324219 to 0.0007324219
- lat2_v: float32 [256, 256], replicated, may hold values from 6.510417e-08 to 2.6041667e-07
- lat3_w: float32 [512, 256], replicated, may hold values from -0.25 to 0.25
- lat3_m: float32 [512, 256], replicated, may hold values from -0.0007324219 to 0.0007324219
- lat3_v: float32 [512, 256], replicated, may hold values from 6.510417e-08 to 2.6041667e-07
- conv_w: float32 [2, 2304, 256], replicated, may hold values from -0.125 to 0.125
- conv_m: float32 [2, 2304, 256], replicated, may hold values from -0.0007324219 to 0.0007324219
- conv_v: float32 [2, 2304, 256], replicated, may hold values from 6.510417e-08 to 2.6041667e-07
- head_w: float32 [257, 12], replicated, may hold values from -0.375 to 0.375
- head_m: float32 [257, 12], replicated, may hold values from -0.00390625 to 0.00390625
- head_v: float32 [257, 12], replicated, may hold values from 1.6276042e-06 to 6.510417e-06
- bias_w: float32 [4, 256], replicated, may hold values from -1.5 to 1.5
- bias_m: float32 [4, 256], replicated, may hold values from -0.0024414062 to 0.0024414062
- bias_v: float32 [4, 256], replicated, may hold values from 5.859375e-07 to 2.34375e-06
Outputs:
- loss: float32 [], replicated
- lat2_new: float32 [256, 256], replicated
- lat2_m_new: float32 [256, 256], replicated
- lat2_v_new: float32 [256, 256], replicated
- lat2_copy: bfloat16 [256, 256], replicated
- lat3_new: float32 [512, 256], replicated
- lat3_m_new: float32 [512, 256], replicated
- lat3_v_new: float32 [512, 256], replicated
- lat3_copy: bfloat16 [512, 256], replicated
- conv_new: float32 [2, 2304, 256], replicated
- conv_m_new: float32 [2, 2304, 256], replicated
- conv_v_new: float32 [2, 2304, 256], replicated
- conv_copy: bfloat16 [2, 2304, 256], replicated
- head_new: float32 [257, 12], replicated
- head_m_new: float32 [257, 12], replicated
- head_v_new: float32 [257, 12], replicated
- head_copy: bfloat16 [257, 12], replicated
- bias_new: float32 [4, 256], replicated
- bias_m_new: float32 [4, 256], replicated
- bias_v_new: float32 [4, 256], replicated
- bias_copy: bfloat16 [4, 256], replicated
The draws below stay inside these ranges and needn't reach their ends.
All inputs are finite; a program needn't handle non-finite values. No bound on the sum of `match2` or of `match3` on one device may be relied on, other than what follows from the above.
Results may differ from the reference program's by a relative error of at most 0.0045.
The reference program's roundings to bfloat16 on the way count: a program that leaves them out, or rounds other values in their place, can miss the bound.
Values may be sent and summed in bfloat16 or wider, within the bound.
A program may use at most 128 MiB of HBM per device.

```python
import math
import jax
import jax.numpy as jnp
from jax import lax

C2 = 256
C3 = 512
FPN = 256
ANCHORS = 3
WIDTH2 = 16
IMAGES = 32
H2 = 64
H3 = 32
W3 = 8
DELTAS = 12
ANCH_ALL = 122880


def place_ends(result, own_key, least, largest):
    longest = result.shape.index(max(result.shape))
    spots = []
    for shift in (0, 1):
        where = [jax.random.randint(jax.random.fold_in(own_key, axis), (), 0, length) for axis, length in enumerate(result.shape)]
        where[longest] = (where[longest] + shift) % result.shape[longest]
        spots.append(tuple(where))
    return result.at[spots[0]].set(least).at[spots[1]].set(largest)


def steps_of(key, shape, cuts, least, top_value):
    factor_of = 1.0
    for dim, parts in cuts:
        draws = jax.random.uniform(jax.random.fold_in(jax.random.fold_in(key, 6), dim), (parts,), jnp.float32, least / len(cuts), top_value / len(cuts))
        factor_of = factor_of * jnp.repeat(jnp.exp(draws), shape[dim] // parts).reshape((-1,) + (1,) * (len(shape) - 1 - dim))
    return factor_of


def scatter_about(stream_key, extent, spread, bound, split=(), dtype=jnp.bfloat16):
    factor_of = steps_of(stream_key, extent, split, -0.22, 0.18) if split else 1.0
    entries = jax.random.normal(stream_key, extent, jnp.float32) * spread * factor_of
    return jnp.minimum(jnp.maximum(entries, -bound), bound).astype(dtype)


def setup_inputs(seed: int = 0) -> dict:
    key_list = jax.random.split(jax.random.key(seed), 24)
    return {
        "feats2": scatter_about(key_list[0], (IMAGES, H2, WIDTH2, C2), 1.0, 6.0, ((0, 4), (1, 8))),
        "feats3": scatter_about(key_list[1], (IMAGES, H3, W3, C3), 1.0, 6.0, ((0, 32),)),
        "match2": place_ends((jax.random.randint(key_list[2], (IMAGES, ANCHORS, H2, WIDTH2), 0, 16) < 1).astype(jnp.int32), jax.random.fold_in(key_list[2], 1), 0, 1),
        "target2": scatter_about(key_list[3], (IMAGES, DELTAS, H2, WIDTH2), 1.0, 6.0, ((0, 4), (2, 8)), jnp.float32),
        "match3": place_ends((jax.random.randint(key_list[4], (IMAGES, ANCHORS, H3, W3), 0, 16) < 1).astype(jnp.int32), jax.random.fold_in(key_list[4], 1), 0, 1),
        "target3": scatter_about(key_list[5], (IMAGES, DELTAS, H3, W3), 1.0, 6.0, ((0, 32),), jnp.float32),
        "positives": jax.random.randint(key_list[6], (), ANCH_ALL // 20, ANCH_ALL // 12).astype(jnp.int32),
        "step_count": jax.random.randint(key_list[7], (), 1, 21).astype(jnp.int32),
        "lat2_w": scatter_about(key_list[8], (C2, FPN), C2 ** -0.5, 0.375, (), jnp.float32),
        "lat2_m": scatter_about(key_list[9], (C2, FPN), (0.011 / (ANCH_ALL // 16) ** 0.5), 0.0007324219, (), jnp.float32),
        "lat2_v": jnp.clip(jnp.exp(jax.random.uniform(key_list[10], (C2, FPN), jnp.float32, math.log(6.510416739047287e-08), math.log(2.6041666956189147e-07))), 6.510416739047287e-08, 2.6041666956189147e-07),
        "lat3_w": scatter_about(key_list[11], (C3, FPN), C3 ** -0.5, 0.25, (), jnp.float32),
        "lat3_m": scatter_about(key_list[12], (C3, FPN), (0.011 / (ANCH_ALL // 16) ** 0.5), 0.0007324219, (), jnp.float32),
        "lat3_v": jnp.clip(jnp.exp(jax.random.uniform(key_list[13], (C3, FPN), jnp.float32, math.log(6.510416739047287e-08), math.log(2.6041666956189147e-07))), 6.510416739047287e-08, 2.6041666956189147e-07),
        "conv_w": scatter_about(key_list[14], (2, 9 * FPN, FPN), (9 * FPN) ** -0.5, 0.125, (), jnp.float32),
        "conv_m": scatter_about(key_list[15], (2, 9 * FPN, FPN), (0.011 / (ANCH_ALL // 16) ** 0.5), 0.0007324219, (), jnp.float32),
        "conv_v": jnp.clip(jnp.exp(jax.random.uniform(key_list[16], (2, 9 * FPN, FPN), jnp.float32, math.log(6.510416739047287e-08), math.log(2.6041666956189147e-07))), 6.510416739047287e-08, 2.6041666956189147e-07),
        "head_w": scatter_about(key_list[17], (FPN + 1, DELTAS), FPN ** -0.5, 0.375, (), jnp.float32),
        "head_m": scatter_about(key_list[18], (FPN + 1, DELTAS), (0.055 / (ANCH_ALL // 16) ** 0.5), 0.00390625, (), jnp.float32),
        "head_v": jnp.clip(jnp.exp(jax.random.uniform(key_list[19], (FPN + 1, DELTAS), jnp.float32, math.log(1.6276042060781037e-06), math.log(6.510416824312415e-06))), 1.6276042060781037e-06, 6.510416824312415e-06),
        "bias_w": scatter_about(key_list[20], (4, FPN), 0.3, 1.5, (), jnp.float32),
        "bias_m": scatter_about(key_list[21], (4, FPN), (0.033 / (ANCH_ALL // 16) ** 0.5), 0.0024414062, (), jnp.float32),
        "bias_v": jnp.clip(jnp.exp(jax.random.uniform(key_list[22], (4, FPN), jnp.float32, math.log(5.859375278305379e-07), math.log(2.3437501113221515e-06))), 5.859375278305379e-07, 2.3437501113221515e-06),
    }


@jax.custom_vjp
def low(v):
    return lax.optimization_barrier(v.astype(jnp.bfloat16)).astype(jnp.float32)

@jax.custom_vjp
def low_back(v):
    return v

def low_keep(v):
    return (low(v), None)

def low_pass(kept, grad):
    return (grad,)

def back_keep(v):
    return (v, None)

def back_low(kept, grad):
    return (low(grad),)
low.defvjp(low_keep, low_pass)
low_back.defvjp(back_keep, back_low)
BETA = 1.0 / 9.0
HIGH = lax.Precision.HIGHEST

def conv_same(inputs, kernel):
    return lax.conv_general_dilated(inputs[None], kernel, (1, 1), ((1, 1), (1, 1)), dimension_numbers=('NHWC', 'HWIO', 'NHWC'), precision=HIGH, preferred_element_type=jnp.float32)[0]

def level_loss(features, head_w, match, target):
    pred = jnp.einsum('hwc,ck->khw', low(features), low(head_w[:-1]), precision=HIGH) + head_w[-1][:, None, None]
    pred = low_back(pred)
    weight = jnp.repeat(match.astype(jnp.float32), 4, axis=0)
    diff = pred - target
    size = jnp.abs(diff)
    return jnp.sum(weight * jnp.where(size < BETA, 0.5 * diff * diff / BETA, size - 0.5 * BETA))

def image_loss(params, feat2, feat3, match2, target2, match3, target3, norm):
    lat2_w, lat3_w, conv_w, head_w, bias_w = params
    width = lat2_w.shape[1]
    kernel = low(conv_w).reshape(2, 3, 3, width, width)
    lateral = low_back(jnp.einsum('hwc,cf->hwf', feat2, low(lat2_w), precision=HIGH) + bias_w[0])
    top = low_back(jnp.einsum('hwc,cf->hwf', feat3, low(lat3_w), precision=HIGH) + bias_w[1])
    top_r = low(top)
    coarse = low_back(conv_same(top_r, kernel[1]) + bias_w[3])
    up_in = low_back(top_r)
    enlarged = jnp.repeat(jnp.repeat(up_in, 2, axis=0), 2, axis=1)
    merged = lateral + enlarged
    fine = low_back(conv_same(low(merged), kernel[0]) + bias_w[2])
    total = level_loss(fine, head_w, match2, target2) + level_loss(coarse, head_w, match3, target3)
    return total / norm

def adamw(weight, first, second, grad, count):
    first_new = 0.9 * first + 0.1 * grad
    second_new = 0.95 * second + 0.05 * grad * grad
    first_hat = first_new / (1.0 - jnp.power(0.9, count))
    second_hat = second_new / (1.0 - jnp.power(0.95, count))
    weight_new = weight - 0.02 * (first_hat / (jnp.sqrt(second_hat) + 1e-08) + 0.1 * weight)
    return (weight_new, first_new, second_new, weight_new.astype(jnp.bfloat16))

def reference(feats2, feats3, match2, target2, match3, target3, positives, step_count, lat2_w, lat2_m, lat2_v, lat3_w, lat3_m, lat3_v, conv_w, conv_m, conv_v, head_w, head_m, head_v, bias_w, bias_m, bias_v):
    params = (lat2_w, lat3_w, conv_w, head_w, bias_w)
    norm = positives.astype(jnp.float32)

    def one(carry, items):
        loss_sum, grads = carry
        feat2, feat3, mk2, tg2, mk3, tg3 = items
        value, pull = jax.vjp(lambda p: image_loss(p, feat2.astype(jnp.float32), feat3.astype(jnp.float32), mk2, tg2, mk3, tg3, norm), params)
        new = pull(jnp.ones((), jnp.float32))[0]
        return ((loss_sum + value, jax.tree.map(lambda a, b: a + b, grads, new)), None)
    start = (jnp.zeros((), jnp.float32), jax.tree.map(jnp.zeros_like, params))
    (loss, grads), unused = lax.scan(one, start, (feats2, feats3, match2, target2, match3, target3))
    count = step_count.astype(jnp.float32)
    outs = [loss]
    for weight, first, second, grad in zip(params, (lat2_m, lat3_m, conv_m, head_m, bias_m), (lat2_v, lat3_v, conv_v, head_v, bias_v), grads):
        outs.extend(adamw(weight, first, second, grad, count))
    return tuple(outs)
```

```python
import functools

import jax
import jax.numpy as jnp
from jax import lax
from jax.experimental import pallas as pl
from jax.experimental.pallas import tpu as pltpu
from jax.sharding import PartitionSpec as P

BETA = 1.0 / 9.0
MESH = pl.DeviceIdType.MESH
VMEM = pltpu.MemorySpace.VMEM
SMEM = pltpu.MemorySpace.SMEM
HBM = pltpu.MemorySpace.HBM
BF = jnp.bfloat16
F32 = jnp.float32
LANES = 128
TAP = 256
BLOCK = 256
TAPS = 21
FINE_JOBS = (
    (range(0, 5), ("x", "b", "a")),
    (range(5, 9), ("b", "x", "a")),
    (range(9, 12), ("x", "ba")),
    (range(12, 15), ("b", "xa")),
    (range(15, 18), ("x", "ba")),
    (range(18, 21), ("b", "xa")),
)
SCHEDULE = {
    "dtop3": (0, 1),
    "target": (),
    "strips": (0, 1),
    "enlarged": (),
    "merged": (),
    "inner": (0, 1),
    "forward": (0, 1),
    "backward": (),
    "conv2a": (),
    "conv2b": (2,),
    "conv2": (0, 1, 3),
    "lat2": (4, 2),
    "lat3": (0, 1, 3, 4, 2, 5),
}
LARGE_JOBS = (
    (range(0, 8), ("x", "b", "a")),
    (range(8, 16), ("b", "x", "a")),
    (range(16, 21), ("x", "b", "a")),
)
TINY = 24


class Plan:
    def __init__(self, mesh_shape, feats2, feats3):
        self.nimg, self.nrow = mesh_shape["img"], mesh_shape["row"]
        self.images, self.rows, self.cols, self.width = feats2
        self.high3, self.cols3, self.width3 = feats3[1:]
        self.strip = self.high3 // self.nrow
        self.lanes = self.images * self.cols
        self.cells3 = self.high3 * self.cols3
        minor = 1
        while minor * minor * 4 <= self.nrow:
            minor *= 2
        self.size = {"c": 2, "x": self.nimg // 2, "b": minor, "a": self.nrow // minor}
        grain = 16 * self.size["x"] * self.nrow
        self.jobs = FINE_JOBS if grain <= TAP else LARGE_JOBS
        self.start, self.length, self.tap_row, self.tap_job = [], [], {}, {}
        row = 0
        for number, (taps, _) in enumerate(self.jobs):
            self.start.append(row)
            for place, tap in enumerate(taps):
                self.tap_row[tap] = row + place * TAP
                self.tap_job[tap] = number
            self.length.append(-(-len(taps) * TAP // grain) * grain)
            row += self.length[-1]
        self.total = row
        self.tiny_links = sum(self.size.values()) - 4
        self.links = 1 + max(
            sum(self.count(group) - 1 for group in order) for _, order in self.jobs
        )

    def count(self, group):
        number = 1
        for dim in group:
            number *= self.size[dim]
        return number


class Place:
    def __init__(self, plan):
        self.plan = plan
        self.img, self.row = lax.axis_index("img"), lax.axis_index("row")
        minor = plan.size["b"]
        self.at = {
            "c": lax.rem(self.img, 2),
            "x": self.img // 2,
            "b": lax.rem(self.row, minor),
            "a": self.row // minor,
        }

    def moved(self, group, distance):
        at = dict(self.at)
        for dim in group[::-1]:
            size = self.plan.size[dim]
            step, distance = distance % size, distance // size
            if step:
                at[dim] = lax.rem(at[dim] + step, size)
        return at

    def coord(self, group, distance=0):
        at = self.moved(group, distance)
        number = 0
        for dim in group:
            number = number * self.plan.size[dim] + at[dim]
        return number

    def peer(self, group, distance):
        at = self.moved(group, distance)
        return (at["x"] * 2 + at["c"], at["a"] * self.plan.size["b"] + at["b"])

    def in_row(self, distance):
        return lax.rem(self.row + distance + self.plan.nrow, self.plan.nrow)


def when(condition, work):
    if condition is None:
        work()
    else:
        pl.when(condition)(work)


class Transfer:
    def __init__(self, copy, remote, out_if=None, in_if=None):
        self.copy, self.remote, self.out_if, self.in_if = copy, remote, out_if, in_if
        self.landed = self.left = False
        when(out_if, copy.start)

    def wait(self):
        if not self.landed:
            when(self.in_if, self.copy.wait_recv if self.remote else self.copy.wait)
        self.landed = True

    def close(self):
        self.wait()
        if self.remote and not self.left:
            when(self.out_if, self.copy.wait_send)
        self.left = True


class Transfers:
    def __init__(self, local, out, into):
        self.local, self.out, self.into = local, out, into
        self.all, self.locals, self.remotes = [], 0, 0

    def load(self, src, dst):
        copy = pltpu.make_async_copy(src, dst, self.local.at[self.locals])
        self.locals += 1
        self.all.append(Transfer(copy, False))
        return self.all[-1]

    def send(self, src, dst, peer, out_if=None, in_if=None):
        copy = pltpu.make_async_remote_copy(
            src_ref=src,
            dst_ref=dst,
            send_sem=self.out.at[self.remotes],
            recv_sem=self.into.at[self.remotes],
            device_id=peer,
            device_id_type=MESH,
        )
        self.remotes += 1
        self.all.append(Transfer(copy, True, out_if, in_if))
        return self.all[-1]

    def close(self):
        for transfer in self.all:
            transfer.close()


def rows_of(count, work, block=640):
    if count <= block or count % block:
        work(0, count)
        return

    def step(index, carry):
        work(pl.multiple_of(index * block, block), block)
        return carry

    lax.fori_loop(0, count // block, step, 0)


class Job:
    def __init__(self, plan, place, number, transfers, bufs, update):
        self.plan, self.place, self.number, self.transfers = plan, place, number, transfers
        self.own, self.send0, self.recv0, self.send, self.recv, self.full = bufs
        self.first, self.length = plan.start[number], plan.length[number]
        taps, self.order = plan.jobs[number]
        self.missing = set(taps)
        self.base, self.size = 0, self.length
        self.regions = []
        self.spare = 0
        self.waiting = []
        self.todo = [self.core] + [functools.partial(self.scatter, group) for group in self.order]
        self.todo += [self.settle]
        self.todo += [functools.partial(self.gather, group) for group in self.order[::-1]]
        self.todo += [self.gather_core, self.arrived]
        self.todo += [functools.partial(update, taps)]

    @property
    def ready(self):
        return not self.missing and bool(self.todo)

    def step(self, steps=1):
        for _ in range(steps):
            if self.ready:
                self.todo.pop(0)()

    def stored(self, tap):
        self.missing.remove(tap)
        if not self.missing:
            self.step()

    def core(self):
        rows = pl.ds(self.first, self.length)
        copy = self.transfers.send(
            self.send0.at[rows], self.recv0.at[rows], self.place.peer("c", 1)
        )
        self.waiting = [(copy, self.recv0, self.first)]

    def arrived(self):
        for copy, _, _ in self.waiting:
            copy.wait()

    def total(self, row, count):
        at = pl.multiple_of(self.first + self.base + row, 16)
        value = self.own[pl.ds(at, count)]
        for _, ref, start in self.waiting:
            value = value + ref[pl.ds(pl.multiple_of(start + row, 16), count)].astype(F32)
        return value

    def scatter(self, group):
        self.arrived()
        size = self.plan.count(group)
        part = self.size // size
        sends = []
        for distance in range(1, size):
            begin = pl.multiple_of(self.place.coord(group, distance) * part, 16)
            spot = self.first + self.spare

            def work(row, count, begin=begin, spot=spot):
                self.send[pl.ds(pl.multiple_of(spot + row, 16), count)] = self.total(
                    pl.multiple_of(begin + row, 16), count
                ).astype(BF)

            rows_of(part, work)
            rows = pl.ds(spot, part)
            copy = self.transfers.send(
                self.send.at[rows], self.recv.at[rows], self.place.peer(group, distance)
            )
            sends.append((copy, self.recv, spot))
            self.spare += part
        begin = pl.multiple_of(self.place.coord(group) * part, 16)

        def keep(row, count):
            here = pl.multiple_of(begin + row, 16)
            value = self.total(here, count)
            self.own[pl.ds(pl.multiple_of(self.first + self.base + here, 16), count)] = value

        rows_of(part, keep)
        self.base = pl.multiple_of(self.base + begin, 16)
        self.size = part
        self.regions.append((self.base, part))
        self.waiting = sends

    def settle(self):
        self.arrived()
        core = self.place.at["c"]

        def work(row, count):
            here = pl.multiple_of(self.first + self.base + row, 16)
            value = self.total(row, count)
            self.full[core, pl.ds(here, count)] = (value * jnp.abs(value)).astype(BF)

        rows_of(self.size, work)
        self.waiting = []
        self.step()

    def gather(self, group):
        self.arrived()
        core = self.place.at["c"]
        base, size = self.regions.pop()
        ref = self.full.at[core, pl.ds(pl.multiple_of(self.first + base, 16), size)]
        self.waiting = [
            (self.transfers.send(ref, ref, self.place.peer(group, distance)), None, None)
            for distance in range(1, self.plan.count(group))
        ]

    def gather_core(self):
        self.arrived()
        core = self.place.at["c"]
        ref = self.full.at[core, pl.ds(self.first, self.length)]
        self.waiting = [(self.transfers.send(ref, ref, self.place.peer("c", 1)), None, None)]


class Tiny:
    def __init__(self, plan, place, transfers, rows, slots, update):
        self.plan, self.place, self.transfers = plan, place, transfers
        self.rows, self.slots = rows, slots
        self.first, self.size, self.waiting = 0, 0, []
        self.todo = [functools.partial(self.share, dim) for dim in "cxba"] + [self.total, update]
        self.ready = False

    def step(self):
        if self.ready and self.todo:
            self.todo.pop(0)()

    def total(self):
        for copy in self.waiting:
            copy.wait()
        if self.waiting:
            self.rows[...] = sum(self.slots[self.first + index] for index in range(self.size))

    def share(self, dim):
        self.total()
        self.first += self.size
        self.size = self.plan.size[dim]
        slot = self.first + self.place.at[dim]
        self.slots[slot] = self.rows[...]
        ref = self.slots.at[slot]
        self.waiting = [
            self.transfers.send(ref, ref, self.place.peer(dim, distance))
            for distance in range(1, self.size)
        ]


def dot(a, b, dims=((1,), (0,))):
    return lax.dot_general(a, b, (dims, ((), ())), preferred_element_type=F32)


NT = ((1,), (1,))
TN = ((0,), (0,))


def shifted(value, period):
    place = lax.rem(lax.broadcasted_iota(jnp.int32, value.shape, 0), period)
    count = value.shape[0]
    on = jnp.where(place == 0, 0.0, pltpu.roll(value, 1, 0)).astype(BF)
    back = jnp.where(place == period - 1, 0.0, pltpu.roll(value, count - 1, 0)).astype(BF)
    return on, back


def level(feat_r, head_t, head_bias, target, weight, norm):
    pred = dot(head_t, feat_r, NT) + head_bias
    diff = pred - target
    size = jnp.abs(diff)
    loss = weight * jnp.where(size < BETA, 0.5 * diff * diff / BETA, size - 0.5 * BETA) / norm
    dpred = (weight * jnp.clip(diff / BETA, -1.0, 1.0) / norm).astype(BF)
    return loss, dpred


ARGS = (
    ("feats2", "feats3", "match2", "target2", "match3", "target3", "positives", "step_count"),
    ("lat2_w", "lat2_m", "lat2_v", "lat3_w", "lat3_m", "lat3_v", "conv_w", "conv_m", "conv_v"),
    ("head_w", "head_m", "head_v", "bias_w", "bias_m", "bias_v"),
)
RESULTS = (
    ("loss", "w2", "m2", "v2", "c2", "w3", "m3", "v3", "c3", "wc", "mc", "vc", "cc"),
    ("wh", "mh", "vh", "ch", "wb", "mb", "vb", "cb"),
)
SCRATCH = (
    ("own", "send0", "recv0", "send", "recv", "full", "tin", "slots"),
    ("f3", "top_s", "top_p", "strips", "x3", "d3", "k3", "t3", "q3", "tp3", "dtop_s"),
    ("f2", "up", "x2", "d2", "p2", "k2", "t2", "q2", "tt", "ww", "edge_o", "edge_i"),
    ("tl", "wl", "dpl", "lossl", "ps", "dup_f", "dup_s", "dup_r", "dm"),
    ("hp", "ht", "w2b", "local_sem", "out_sem", "in_sem"),
)


class Refs:
    def __init__(self, groups, refs):
        names = [name for group in groups for name in group]
        self.__dict__.update(zip(names, refs, strict=True))


def adamw(weight, first, second, grad, square, scale1, scale2):
    first_new = 0.9 * first + 0.1 * grad
    second_new = 0.95 * second + 0.05 * square
    weight_new = weight - 0.02 * (
        first_new * scale1 / (jnp.sqrt(second_new * scale2) + 1e-08) + 0.1 * weight
    )
    return weight_new, first_new, second_new


def main_kernel(plan, *refs):
    g = Refs(ARGS + RESULTS + SCRATCH, refs)
    place = Place(plan)
    me = place.row
    C, L = plan.width, plan.lanes
    images, rows, cols = plan.images, plan.rows, plan.cols
    H3, W3, strip = plan.high3, plan.cols3, plan.strip
    nrow = plan.nrow

    barrier = pltpu.get_barrier_semaphore()
    greeted = 0
    for distance in range(1, nrow):
        pl.semaphore_signal(
            barrier, inc=1, device_id=(place.img, place.in_row(distance)), device_id_type=MESH
        )
        greeted += 1
    for dim in "cx":
        for distance in range(1, plan.size[dim]):
            pl.semaphore_signal(
                barrier, inc=1, device_id=place.peer(dim, distance), device_id_type=MESH
            )
            greeted += 1

    transfers = Transfers(g.local_sem, g.out_sem, g.in_sem)
    load = transfers.load
    load_f3 = load(g.feats3, g.f3)
    load_w3 = load(g.lat3_w, g.w3)
    load_bias = load(g.bias_w, g.wb)
    load_head = load(g.head_w, g.wh)
    load_t3 = [load(g.target3.at[0], g.t3), load(g.match3.at[0], g.q3)]

    norm = g.positives[0].astype(F32)
    count = jnp.full((1, LANES), g.step_count[0].astype(F32))
    scale1 = (1.0 / (1.0 - jnp.exp(count * jnp.log(jnp.float32(0.9)))))[:, 0:1]
    scale2 = (1.0 / (1.0 - jnp.exp(count * jnp.log(jnp.float32(0.95)))))[:, 0:1]

    g.top_s[:, 0:8] = jnp.zeros((2, 8, LANES), F32)
    g.top_s[:, 8 + plan.cells3 : 16 + plan.cells3] = jnp.zeros((2, 8, LANES), F32)
    for ref in (g.x3, g.d3):
        ref[0] = jnp.zeros((H3, 3 * C), BF)
        ref[W3 + 1] = jnp.zeros((H3, 3 * C), BF)
    g.hp[...] = jnp.zeros(g.hp.shape, F32)
    for job, (taps, _) in enumerate(plan.jobs):
        used = len(taps) * TAP
        spare = plan.length[job] - used
        if spare:
            at = pl.ds(plan.start[job] + used, spare)
            g.own[at] = jnp.zeros((spare, LANES), F32)
            g.send0[at] = jnp.zeros((spare, LANES), BF)

    load_f3.wait()
    load_w3.wait()
    load_bias.wait()
    load_c3 = load(g.conv_w.at[1], g.wc.at[1])
    load_f2 = [load(g.feats2.at[:, f], g.f2.at[2 + f]) for f in range(rows)]
    load_w2 = load(g.lat2_w, g.w2)
    load_t2 = [load(g.target2, g.t2), load(g.match2, g.q2)]
    load_c2 = load(g.conv_w.at[0], g.wc.at[0])
    top = dot(g.f3[...], g.w3[...].astype(BF)) + g.wb[1:2]
    top = top.astype(BF).astype(F32)
    for half in range(2):
        g.top_s[half, 8 : 8 + plan.cells3] = top[:, half * LANES : (half + 1) * LANES]
    for half in range(2):
        g.top_p[:, half * LANES : (half + 1) * LANES] = g.top_s[half].astype(BF)
    pl.semaphore_wait(barrier, greeted)
    span = (strip + 2) * W3
    strip_sends = []
    for distance in range(1, nrow):
        other = place.in_row(distance)
        src = g.top_p.at[pl.ds(pl.multiple_of(other * strip * W3, 16), span)]
        strip_sends.append(transfers.send(src, g.strips.at[me], (place.img, other)))
    g.strips[me] = g.top_p[pl.ds(pl.multiple_of(me * strip * W3, 16), span)]

    has_up, has_down = me > 0, me < nrow - 1
    up_dev, down_dev = (place.img, me - 1), (place.img, me + 1)
    edge_f2 = []
    for f in range(2):
        edge_f2.append(
            transfers.send(g.feats2.at[:, f], g.f2.at[rows + 2 + f], up_dev, has_up, has_down)
        )
    for f in range(2):
        edge_f2.append(
            transfers.send(g.feats2.at[:, rows - 2 + f], g.f2.at[f], down_dev, has_down, has_up)
        )


    value = jnp.concatenate(
        [
            jnp.concatenate(
                [g.top_s[half, pl.ds(8 + col, H3, stride=W3), :] for half in range(2)], axis=1
            )
            for col in range(W3)
        ],
        axis=0,
    )

    def three(ref, low, middle, high):
        for at, value in enumerate((low, middle, high)):
            ref[1 : W3 + 1, :, at * C : (at + 1) * C] = value.reshape(W3, H3, C)

    on, back = shifted(value, H3)
    three(g.x3, on, value.astype(BF), back)
    load_c3.wait()
    for dx in range(3):
        for dy in range(3):
            tap = dy * 3 + dx
            g.k3[dx, dy * C : (dy + 1) * C] = g.wc[1, tap * C : (tap + 1) * C].astype(BF)
    load_head.wait()
    g.hp[0:12, 0 : C + 1] = g.wh[...]
    g.ht[...] = g.hp[:, 0:C].astype(BF)
    head_bias = g.hp[:, C : C + 1]
    head_t = g.ht[...]

    for copy in load_t3:
        copy.wait()
    g.tp3[...] = jnp.zeros(g.tp3.shape, F32)
    for k in range(12):
        g.tp3[0, k * W3 : (k + 1) * W3, 0:H3] = g.t3[k]
        g.tp3[1, k * W3 : (k + 1) * W3, 0:H3] = g.q3[k // 4].astype(F32)

    def coarse_rows(which):
        return jnp.concatenate(
            [g.tp3[which, pl.ds(col, 16, stride=W3), :][:, 0:H3] for col in range(W3)], axis=1
        )

    target3, weight3 = coarse_rows(0), coarse_rows(1)

    def window3(ref, dx):
        return ref[dx : dx + W3].reshape(plan.cells3, 3 * C)

    coarse = g.wb[3:4] + dot(
        jnp.concatenate([window3(g.x3, dx) for dx in range(3)], axis=1),
        g.k3[...].reshape(9 * C, C),
    )
    coarse_r = coarse.astype(BF)
    loss3, dpred3 = level(coarse_r, head_t, head_bias, target3, weight3, norm)
    head_g = dot(dpred3, coarse_r)
    hbias_g = jnp.sum(dpred3.astype(F32), axis=1, keepdims=True)
    loss = jnp.sum(loss3, axis=1, keepdims=True)
    dcoarse_r = dot(dpred3, head_t, TN).astype(BF)
    out_g3 = jnp.sum(dcoarse_r.astype(F32), axis=0, keepdims=True)
    g.tin[0:16] = head_g
    g.tin[19:20] = out_g3
    on, back = shifted(dcoarse_r.astype(F32), H3)
    three(g.d3, back, dcoarse_r, on)
    core = place.at["c"]

    arrays = {0: (g.wc, g.mc, g.vc, g.cc, 1), 9: (g.wc, g.mc, g.vc, g.cc, 0)}
    arrays |= {18: (g.w2, g.m2, g.v2, g.c2, None), 19: (g.w3, g.m3, g.v3, g.c3, None)}

    def update(taps):
        runs = []
        for tap in taps:
            first = max(start for start in arrays if start <= tap)
            if runs and runs[-1][0] == first:
                runs[-1][2] += TAP
            else:
                runs.append([first, tap, TAP])
        for first, tap, length in runs:
            *held, lead = arrays[first]

            def block(index, carry, first=first, tap=tap, held=held, lead=lead):
                row = pl.multiple_of(plan.tap_row[tap] + index * BLOCK, BLOCK)
                at = pl.ds(pl.multiple_of((tap - first) * TAP + index * BLOCK, BLOCK), BLOCK)
                for half in range(2):
                    lanes = slice(half * LANES, (half + 1) * LANES)
                    where = (at, lanes) if lead is None else (lead, at, lanes)
                    signed = g.full[half, pl.ds(row, BLOCK)].astype(F32)
                    square = jnp.abs(signed)
                    grad = jnp.sqrt(square)
                    grad = jnp.where(signed < 0.0, -grad, grad)
                    old = [ref[where] for ref in held[:3]]
                    new = adamw(*old, grad, square, scale1, scale2)
                    for ref, value in zip(held, new):
                        ref[where] = value
                    held[3][where] = new[0].astype(BF)
                return carry

            lax.fori_loop(0, length // BLOCK, block, 0)

    bufs = (g.own, g.send0, g.recv0, g.send, g.recv, g.full)
    jobs = [
        Job(plan, place, number, transfers, bufs, update) for number in range(len(plan.jobs))
    ]

    def progress(point):
        for number in SCHEDULE[point]:
            if number < len(jobs):
                jobs[number].step()

    def store_tap(tap, value):
        at = pl.ds(plan.tap_row[tap], TAP)
        left, right = value[:, 0:LANES], value[:, LANES:]
        mine = core == 0
        g.own[at] = jnp.where(mine, left, right)
        g.send0[at] = jnp.where(mine, right, left).astype(BF)
        jobs[plan.tap_job[tap]].stored(tap)

    for dx in range(3):
        grad = dot(window3(g.x3, dx), dcoarse_r, TN)
        for dy in range(3):
            store_tap(dy * 3 + dx, grad[dy * C : (dy + 1) * C])

    dtop = sum(
        dot(window3(g.d3, 2 - dx)[:, dy * C : (dy + 1) * C], g.k3[dx, dy * C : (dy + 1) * C], NT)
        for dx in range(3)
        for dy in range(3)
    )
    for col in range(W3):
        for half in range(2):
            g.dtop_s[half, pl.ds(col, H3, stride=W3), :] = dtop[
                col * H3 : (col + 1) * H3, half * LANES : (half + 1) * LANES
            ]

    late = [
        load(src, dst)
        for src, dst in (
            (g.lat2_m, g.m2),
            (g.lat2_v, g.v2),
            (g.lat3_m, g.m3),
            (g.lat3_v, g.v3),
            (g.conv_m, g.mc),
            (g.conv_v, g.vc),
            (g.head_m, g.mh),
            (g.head_v, g.vh),
            (g.bias_m, g.mb),
            (g.bias_v, g.vb),
        )
    ]

    progress("dtop3")

    for copy in load_t2:
        copy.wait()
    per = LANES // cols
    for part in range(L // LANES):
        g.tt[part] = jnp.zeros(g.tt.shape[1:], F32)
        g.ww[part] = jnp.zeros(g.ww.shape[1:], F32)
        for k in range(12):
            g.tt[part, k * rows : (k + 1) * rows] = jnp.concatenate(
                [g.t2[part * per + n, k] for n in range(per)], axis=1
            )
        for anchor in range(3):
            value = jnp.concatenate(
                [g.q2[part * per + n, anchor] for n in range(per)], axis=1
            ).astype(F32)
            for k in range(anchor * 4, anchor * 4 + 4):
                g.ww[part, k * rows : (k + 1) * rows] = value
        lanes = slice(part * LANES, (part + 1) * LANES)
        for f in range(rows):
            at = pl.ds(f, 16, stride=rows)
            g.tl[1 + f, :, lanes] = g.tt[part, at, :]
            g.wl[1 + f, :, lanes] = g.ww[part, at, :]
    g.edge_o[0, 0:16] = g.tl[1]
    g.edge_o[0, 16:32] = g.wl[1]
    g.edge_o[1, 0:16] = g.tl[rows]
    g.edge_o[1, 16:32] = g.wl[rows]

    edge_up = transfers.send(g.edge_o.at[0], g.edge_i.at[0], up_dev, has_up, has_down)
    edge_down = transfers.send(g.edge_o.at[1], g.edge_i.at[1], down_dev, has_down, has_up)
    progress("target")

    load_w2.wait()
    g.w2b[...] = g.w2[...].astype(BF)
    load_c2.wait()

    g.k2[...] = g.wc[0].astype(BF)

    for copy in load_f2:
        copy.wait()
    for copy in strip_sends:
        copy.wait()
    progress("strips")
    place_i = lax.broadcasted_iota(jnp.int32, ((strip + 2) * cols, span), 0)
    place_j = lax.broadcasted_iota(jnp.int32, ((strip + 2) * cols, span), 1)
    double = jnp.where(place_i // (cols // W3) == place_j, 1.0, 0.0).astype(BF)

    for n in range(images):
        value = dot(double, g.strips[n])
        for cr in range(strip + 2):
            g.up[cr, n] = value[cr * cols : (cr + 1) * cols]
    progress("enlarged")

    def merge(first, count, outside):
        lateral = dot(g.f2[first : first + count].reshape(count * L, C), g.w2b[...]) + g.wb[0:1]
        value = lateral + jnp.concatenate(
            [g.up[j // 2].reshape(L, C) for j in range(first, first + count)], axis=0
        )
        if outside is not None:
            value = jnp.where(outside, 0.0, value)
        value = value.astype(BF)
        on, back = shifted(value.astype(F32), cols)
        for at, part in enumerate((on, value, back)):
            g.x2[first : first + count, :, at * C : (at + 1) * C] = part.reshape(count, L, C)

    def forward(spans):
        lines = [j for first, count in spans for j in range(first, first + count)]
        cells = len(lines) * L
        fine = g.wb[2:3] + dot(
            jnp.concatenate(
                [
                    jnp.concatenate(
                        [g.x2[first + dy : first + dy + count] for first, count in spans], axis=0
                    ).reshape(cells, 3 * C)
                    for dy in range(3)
                ],
                axis=1,
            ),
            g.k2[...],
        )
        fine_r = fine.astype(BF)
        target = jnp.concatenate([g.tl[j] for j in lines], axis=1)
        weight = jnp.concatenate([g.wl[j] for j in lines], axis=1)
        loss2, dpred = level(fine_r, head_t, head_bias, target, weight, norm)
        value = dot(dpred, head_t, TN).astype(BF)
        on, back = shifted(value.astype(F32), cols)
        for at, j in enumerate(lines):
            here = slice(at * L, (at + 1) * L)
            g.p2[j] = fine_r[here]
            g.lossl[j] = loss2[:, here]
            g.dpl[j] = dpred[:, here]
            for side, part in enumerate((back, value, on)):
                g.d2[j, :, side * C : (side + 1) * C] = part[here]

    merge(2, rows, None)
    progress("merged")
    forward([(2, rows - 2)])
    progress("inner")
    for copy in edge_f2 + [edge_up, edge_down]:
        copy.wait()

    @pl.when(has_up)
    def _():
        g.tl[0] = g.edge_i[1, 0:16]
        g.wl[0] = g.edge_i[1, 16:32]

    @pl.when(me == 0)
    def _():
        g.f2[0:2] = jnp.zeros((2, images, cols, C), BF)
        g.tl[0] = jnp.zeros((16, L), F32)
        g.wl[0] = jnp.zeros((16, L), F32)

    @pl.when(has_down)
    def _():
        g.tl[rows + 1] = g.edge_i[0, 0:16]
        g.wl[rows + 1] = g.edge_i[0, 16:32]

    @pl.when(me == nrow - 1)
    def _():
        g.f2[rows + 2 : rows + 4] = jnp.zeros((2, images, cols, C), BF)
        g.tl[rows + 1] = jnp.zeros((16, L), F32)
        g.wl[rows + 1] = jnp.zeros((16, L), F32)


    merge(0, 2, me == 0)
    merge(rows + 2, 2, me == nrow - 1)
    forward([(0, 2), (rows, 2)])
    progress("forward")

    total = sum(
        dot(
            g.d2[2 - dy : 2 - dy + rows].reshape(rows * L, 3 * C)[:, dx * C : (dx + 1) * C],
            g.k2[(dy * 3 + dx) * C : (dy * 3 + dx + 1) * C],
            NT,
        )
        for dy in range(3)
        for dx in range(3)
    )
    g.dm[...] = total.astype(BF).reshape(rows, L, C)
    for q in range(strip):
        pair = total[2 * q * L : (2 * q + 1) * L] + total[(2 * q + 1) * L : (2 * q + 2) * L]
        for half in range(2):
            g.ps[q, half] = pair[:, half * LANES : (half + 1) * LANES]
            value = (
                g.ps[q, half, pl.ds(0, L // 2, stride=2), :]
                + g.ps[q, half, pl.ds(1, L // 2, stride=2), :]
            )
            g.dup_f[:, q * W3 : (q + 1) * W3, half * LANES : (half + 1) * LANES] = value.reshape(
                images, W3, LANES
            )
    g.dup_s[...] = g.dup_f[...].astype(BF)
    dup_sends = []
    for distance in range(1, nrow):
        other = place.in_row(distance)
        dup_sends.append(transfers.send(g.dup_s.at[other], g.dup_r.at[me], (place.img, other)))
    g.dup_r[me] = g.dup_s[me]
    progress("backward")

    inner = g.d2[1 : rows + 1][:, :, C : 2 * C].reshape(rows * L, C)
    for dy in range(3):
        grad = dot(g.x2[dy + 1 : dy + 1 + rows].reshape(rows * L, 3 * C), inner, TN)
        for dx in range(3):
            store_tap(9 + dy * 3 + dx, grad[dx * C : (dx + 1) * C])
        progress(("conv2a", "conv2b", "conv2")[dy])

    dpred2 = jnp.concatenate([g.dpl[1 + f] for f in range(rows)], axis=1)
    g.tin[0:16] += dot(dpred2, g.p2[1 : rows + 1].reshape(rows * L, C))
    hbias_g += jnp.sum(dpred2.astype(F32), axis=1, keepdims=True)
    loss += jnp.sum(sum(g.lossl[1 + f] for f in range(rows)), axis=1, keepdims=True)
    lane = lax.broadcasted_iota(jnp.int32, (16, LANES), 1)
    diagonal = lane == lax.broadcasted_iota(jnp.int32, (16, LANES), 0)
    g.tin[20:21, 0:LANES] = jnp.sum(jnp.where(diagonal, hbias_g, 0.0), axis=0, keepdims=True)
    g.tin[20:21, LANES:] = jnp.sum(
        jnp.broadcast_to(loss, (16, LANES)), axis=0, keepdims=True
    )
    g.tin[18:19] = jnp.sum(inner.astype(F32), axis=0, keepdims=True)
    g.tin[21:24] = jnp.zeros((3, C), F32)
    dm = g.dm[...].reshape(rows * L, C)
    store_tap(18, dot(g.f2[2 : rows + 2].reshape(rows * L, C), dm, TN))
    g.tin[16:17] = jnp.sum(dm.astype(F32), axis=0, keepdims=True)
    progress("lat2")

    for copy in dup_sends:
        copy.wait()
    dup = g.dup_r[...].reshape(plan.cells3, C).astype(F32)
    dtop = jnp.concatenate([g.dtop_s[0], g.dtop_s[1]], axis=1) + dup
    dtop_r = dtop.astype(BF)
    lat3_g = dot(g.f3[...], dtop_r, TN)
    store_tap(19, lat3_g[0:TAP])
    store_tap(20, lat3_g[TAP:])
    g.tin[17:18] = jnp.sum(dtop_r.astype(F32), axis=0, keepdims=True)
    progress("lat3")

    for copy in late:
        copy.wait()

    def update_tiny():
        hbias = jnp.sum(
            jnp.where(diagonal, jnp.broadcast_to(g.tin[20:21, 0:LANES], (16, LANES)), 0.0),
            axis=1,
            keepdims=True,
        )
        grad = jnp.concatenate([g.tin[0:12], hbias[0:12]], axis=1)
        new = adamw(g.wh[...], g.mh[...], g.vh[...], grad, grad * grad, scale1, scale2)
        for ref, value in zip((g.wh, g.mh, g.vh), new):
            ref[...] = value
        g.ch[...] = new[0].astype(BF)
        grad = g.tin[16:20]
        new = adamw(g.wb[...], g.mb[...], g.vb[...], grad, grad * grad, scale1, scale2)
        for ref, value in zip((g.wb, g.mb, g.vb), new):
            ref[...] = value
        g.cb[...] = new[0].astype(BF)
        g.loss[...] = g.tin[16:24, LANES:]

    small = Tiny(plan, place, transfers, g.tin, g.slots, update_tiny)
    small.ready = True
    while any(job.todo for job in jobs + [small]):
        small.step()
        for job in jobs:
            job.step()
    transfers.close()


def write_kernel(*refs):
    ins, outs, sem = refs[:21], refs[21:42], refs[42]
    copies = []
    for index in range(1, 21):
        src, dst = ins[index], outs[index]
        pairs = [(src, dst)]
        if len(src.shape) == 3:
            pairs = [(src.at[level], dst.at[level]) for level in range(src.shape[0])]
        for pair in pairs:
            copies.append(pltpu.make_async_copy(*pair, sem.at[len(copies)]))
            copies[-1].start()
    outs[0][0] = jnp.max(ins[0][4:5])
    for copy in copies:
        copy.wait()


def body(
    mesh_shape,
    feats2,
    feats3,
    match2,
    target2,
    match3,
    target3,
    positives,
    step_count,
    lat2_w,
    lat2_m,
    lat2_v,
    lat3_w,
    lat3_m,
    lat3_v,
    conv_w,
    conv_m,
    conv_v,
    head_w,
    head_m,
    head_v,
    bias_w,
    bias_m,
    bias_v,
):
    plan = Plan(mesh_shape, feats2.shape, feats3.shape)
    C, L, H3, W3 = plan.width, plan.lanes, plan.high3, plan.cols3
    images, rows, cols, strip, nrow = plan.images, plan.rows, plan.cols, plan.strip, plan.nrow
    head = [x.T for x in (head_w, head_m, head_v)]
    weights = [lat2_w, lat2_m, lat2_v, lat3_w, lat3_m, lat3_v, conv_w, conv_m, conv_v]
    weights += head + [bias_w, bias_m, bias_v]
    args = [
        feats2,
        feats3.reshape(plan.cells3, plan.width3),
        match2,
        target2,
        match3.transpose(0, 1, 3, 2),
        target3.transpose(0, 1, 3, 2),
    ]
    args = [pltpu.with_memory_space_constraint(x, HBM) for x in args]
    held = [pltpu.with_memory_space_constraint(x, HBM) for x in weights]
    hbm, vmem, smem = (pl.BlockSpec(memory_space=space) for space in (HBM, VMEM, SMEM))
    outs = [VMEM((8, LANES), F32)]
    for x in (lat2_w, lat3_w, conv_w, head[0], bias_w):
        outs += [VMEM(x.shape, F32)] * 3 + [VMEM(x.shape, BF)]
    span = (strip + 2) * W3
    dma = pltpu.SemaphoreType.DMA
    remotes = 2 * (nrow - 1) + 6 + plan.tiny_links + len(plan.jobs) * 2 * plan.links
    scratch = [
        VMEM((plan.total, LANES), F32),
        VMEM((plan.total, LANES), BF),
        VMEM((plan.total, LANES), BF),
        VMEM((plan.total, LANES), BF),
        VMEM((plan.total, LANES), BF),
        VMEM((2, plan.total, LANES), BF),
        VMEM((TINY, C), F32),
        VMEM((sum(plan.size.values()), TINY, C), F32),
        VMEM((plan.cells3, plan.width3), BF),
        VMEM((2, plan.cells3 + 16, LANES), F32),
        VMEM((plan.cells3 + 16, C), BF),
        VMEM((nrow, span, C), BF),
        VMEM((W3 + 2, H3, 3 * C), BF),
        VMEM((W3 + 2, H3, 3 * C), BF),
        VMEM((3, 3 * C, C), BF),
        VMEM((12, W3, H3), F32),
        VMEM((3, W3, H3), jnp.int32),
        VMEM((2, 16 * W3, LANES), F32),
        VMEM((2, plan.cells3, LANES), F32),
        VMEM((rows + 4, images, cols, C), BF),
        VMEM((strip + 2, images, cols, C), F32),
        VMEM((rows + 4, L, 3 * C), BF),
        VMEM((rows + 2, L, 3 * C), BF),
        VMEM((rows + 2, L, C), BF),
        VMEM((9 * C, C), BF),
        VMEM(target2.shape, F32),
        VMEM(match2.shape, jnp.int32),
        VMEM((L // LANES, 16 * rows, LANES), F32),
        VMEM((L // LANES, 16 * rows, LANES), F32),
        VMEM((2, 32, L), F32),
        VMEM((2, 32, L), F32),
        VMEM((rows + 2, 16, L), F32),
        VMEM((rows + 2, 16, L), F32),
        VMEM((rows + 2, 16, L), BF),
        VMEM((rows + 2, 16, L), F32),
        VMEM((strip, 2, L, LANES), F32),
        VMEM((images, strip * W3, C), F32),
        VMEM((images, strip * W3, C), BF),
        VMEM((nrow, strip * W3, C), BF),
        VMEM((rows, L, C), BF),
        VMEM((16, 3 * LANES), F32),
        VMEM((16, C), BF),
        VMEM((C, C), BF),
        dma((48,)),
        dma((remotes,)),
        dma((remotes,)),
    ]
    results = pl.pallas_call(
        functools.partial(main_kernel, plan),
        out_shape=outs,
        in_specs=[hbm] * 6 + [smem] * 2 + [hbm] * len(held),
        out_specs=[vmem] * len(outs),
        scratch_shapes=scratch,
        compiler_params=pltpu.CompilerParams(
            collective_id=0, has_side_effects=True, vmem_limit_bytes=40 << 20
        ),
        name="gradients",
    )(*args, positives.reshape(1), step_count.reshape(1), *held)
    kept = [pltpu.with_memory_space_constraint(x, VMEM) for x in results]

    shapes = [jax.ShapeDtypeStruct((1,), F32)]
    shapes += [jax.ShapeDtypeStruct(x.shape, x.dtype) for x in kept[1:]]
    new = pl.pallas_call(
        write_kernel,
        out_shape=shapes,
        in_specs=[vmem] * len(kept),
        out_specs=[smem] + [hbm] * 20,
        scratch_shapes=[dma((24,))],
        compiler_params=pltpu.CompilerParams(vmem_limit_bytes=1 << 20),
        name="results",
    )(*kept)
    outs = [new[0].reshape(())] + list(new[1:])
    for index in range(13, 17):
        outs[index] = outs[index].T
    return tuple(outs)


def solution(mesh):
    split = (
        P("img", "row", None, None),
        P(("img", "row"), None, None, None),
        P("img", None, "row", None),
        P("img", None, "row", None),
        P(("img", "row"), None, None, None),
        P(("img", "row"), None, None, None),
    )
    return jax.shard_map(
        functools.partial(body, dict(mesh.shape)),
        mesh=mesh,
        in_specs=split + (P(),) * 17,
        out_specs=(P(),) * 21,
        check_vma=False,
    )
```

```python
import functools

import jax
import jax.numpy as jnp
from jax import lax
from jax.experimental import pallas as pl
from jax.experimental.pallas import tpu as pltpu
from jax.sharding import PartitionSpec as P

BETA = 1.0 / 9.0
MESH = pl.DeviceIdType.MESH
VMEM = pltpu.MemorySpace.VMEM
SMEM = pltpu.MemorySpace.SMEM
HBM = pltpu.MemorySpace.HBM
BF = jnp.bfloat16
F32 = jnp.float32
LANES = 128
TAP = 256
BLOCK = 256
TAPS = 21
FINE_JOBS = ((range(0,5),('xb', 'a')),(range(5,9),('xb', 'a')),(range(9,12),('xb', 'a')),(range(12,15),('xb', 'a')),(range(15,18),('xb', 'a')),(range(18,21),('xb', 'a')),)
SCHEDULE = {'dtop3': '', 'target': '01', 'strips': '', 'enlarged': '', 'merged': '', 'inner': '', 'forward': '', 'backward': '', 'conv2a': '', 'conv2b': '0', 'conv2': '23', 'lat2': '14', 'lat3': 'tt5021t34t02513tt420530145212334545'}
LARGE_JOBS = (
    (range(0, 8), ("x", "b", "a")),
    (range(8, 16), ("b", "x", "a")),
    (range(16, 21), ("x", "b", "a")),
)
TINY = 24


class Plan:
    def __init__(self, mesh_shape, feats2, feats3):
        self.nimg, self.nrow = mesh_shape["img"], mesh_shape["row"]
        self.images, self.rows, self.cols, self.width = feats2
        self.high3, self.cols3, self.width3 = feats3[1:]
        self.strip = self.high3 // self.nrow
        self.lanes = self.images * self.cols
        self.cells3 = self.high3 * self.cols3
        minor = 1
        while minor * minor * 4 <= self.nrow:
            minor *= 2
        self.size = {"c": 2, "x": self.nimg // 2, "b": minor, "a": self.nrow // minor}
        grain = 16 * self.size["x"] * self.nrow
        self.jobs = FINE_JOBS if grain <= TAP else LARGE_JOBS
        self.start, self.length, self.tap_row, self.tap_job = [], [], {}, {}
        row = 0
        for number, (taps, _) in enumerate(self.jobs):
            self.start.append(row)
            for place, tap in enumerate(taps):
                self.tap_row[tap] = row + place * TAP
                self.tap_job[tap] = number
            self.length.append(-(-len(taps) * TAP // grain) * grain)
            row += self.length[-1]
        self.total = row
        self.tiny_links = sum(self.size.values()) - 4
        self.links = 1 + max(
            sum(self.count(group) - 1 for group in order) for _, order in self.jobs
        )

    def count(self, group):
        number = 1
        for dim in group:
            number *= self.size[dim]
        return number

    def crosses(self, group, distance):
        moved = set()
        for dim in group[::-1]:
            step, distance = distance % self.size[dim], distance // self.size[dim]
            if step:
                moved.add(dim)
        return "x" in moved and len(moved) > 1


class Place:
    def __init__(self, plan):
        self.plan = plan
        self.img, self.row = lax.axis_index("img"), lax.axis_index("row")
        minor = plan.size["b"]
        self.at = {
            "c": lax.rem(self.img, 2),
            "x": self.img // 2,
            "b": lax.rem(self.row, minor),
            "a": self.row // minor,
        }

    def moved(self, group, distance):
        at = dict(self.at)
        for dim in group[::-1]:
            size = self.plan.size[dim]
            step, distance = distance % size, distance // size
            if step:
                at[dim] = lax.rem(at[dim] + step, size)
        return at

    def coord(self, group, distance=0):
        at = self.moved(group, distance)
        number = 0
        for dim in group:
            number = number * self.plan.size[dim] + at[dim]
        return number

    def peer(self, group, distance):
        at = self.moved(group, distance)
        return (at["x"] * 2 + at["c"], at["a"] * self.plan.size["b"] + at["b"])

    def in_row(self, distance):
        return lax.rem(self.row + distance + self.plan.nrow, self.plan.nrow)


def when(condition, work):
    if condition is None:
        work()
    else:
        pl.when(condition)(work)


class Transfer:
    def __init__(self, copy, remote, out_if=None, in_if=None):
        self.copy, self.remote, self.out_if, self.in_if = copy, remote, out_if, in_if
        self.landed = self.left = False
        when(out_if, copy.start)

    def wait(self):
        if not self.landed:
            when(self.in_if, self.copy.wait_recv if self.remote else self.copy.wait)
        self.landed = True

    def close(self):
        self.wait()
        if self.remote and not self.left:
            when(self.out_if, self.copy.wait_send)
        self.left = True


class Transfers:
    def __init__(self, local, out, into):
        self.local, self.out, self.into = local, out, into
        self.all, self.locals, self.remotes = [], 0, 0

    def load(self, src, dst):
        copy = pltpu.make_async_copy(src, dst, self.local.at[self.locals])
        self.locals += 1
        self.all.append(Transfer(copy, False))
        return self.all[-1]

    def send(self, src, dst, peer, out_if=None, in_if=None):
        copy = pltpu.make_async_remote_copy(
            src_ref=src,
            dst_ref=dst,
            send_sem=self.out.at[self.remotes],
            recv_sem=self.into.at[self.remotes],
            device_id=peer,
            device_id_type=MESH,
        )
        self.remotes += 1
        self.all.append(Transfer(copy, True, out_if, in_if))
        return self.all[-1]

    def close(self):
        for transfer in self.all:
            transfer.close()


def rows_of(count, work, block=640):
    if count <= block or count % block:
        work(0, count)
        return

    def step(index, carry):
        work(pl.multiple_of(index * block, block), block)
        return carry

    lax.fori_loop(0, count // block, step, 0)


class Job:
    def __init__(self, plan, place, number, transfers, bufs, update):
        self.plan, self.place, self.number, self.transfers = plan, place, number, transfers
        self.own, self.send0, self.recv0, self.send, self.recv, self.full = bufs
        self.first, self.length = plan.start[number], plan.length[number]
        taps, self.order = plan.jobs[number]
        self.missing = set(taps)
        self.base, self.size = 0, self.length
        self.regions = []
        self.spare = 0
        self.waiting = []
        self.todo = [self.core] + [functools.partial(self.scatter, group) for group in self.order]
        self.todo += [self.settle]
        self.todo += [functools.partial(self.gather, group) for group in self.order[::-1]]
        self.todo += [self.gather_core, functools.partial(self.finish, update, taps)]

    @property
    def ready(self):
        return not self.missing and bool(self.todo)

    def step(self, steps=1):
        for _ in range(steps):
            if self.ready:
                self.todo.pop(0)()

    def stored(self, tap):
        self.missing.remove(tap)
        if not self.missing:
            self.step()

    def core(self):
        rows = pl.ds(self.first, self.length)
        copy = self.transfers.send(
            self.send0.at[rows], self.recv0.at[rows], self.place.peer("c", 1)
        )
        self.waiting = [(copy, self.recv0, self.first)]

    def arrived(self):
        for copy, _, _ in self.waiting:
            copy.wait()

    def finish(self, update, taps):
        self.arrived()
        update(taps)

    def total(self, row, count):
        at = pl.multiple_of(self.first + self.base + row, 16)
        value = self.own[pl.ds(at, count)]
        for _, ref, start in self.waiting:
            value = value + ref[pl.ds(pl.multiple_of(start + row, 16), count)].astype(F32)
        return value

    def scatter(self, group):
        self.arrived()
        size = self.plan.count(group)
        part = self.size // size
        sends = []
        for distance in range(1, size):
            begin = pl.multiple_of(self.place.coord(group, distance) * part, 16)
            spot = self.first + self.spare

            def work(row, count, begin=begin, spot=spot):
                self.send[pl.ds(pl.multiple_of(spot + row, 16), count)] = self.total(
                    pl.multiple_of(begin + row, 16), count
                ).astype(BF)

            rows_of(part, work)
            rows = pl.ds(spot, part)
            copy = self.transfers.send(
                self.send.at[rows], self.recv.at[rows], self.place.peer(group, distance)
            )
            sends.append((copy, self.recv, spot))
            self.spare += part
        begin = pl.multiple_of(self.place.coord(group) * part, 16)

        def keep(row, count):
            here = pl.multiple_of(begin + row, 16)
            value = self.total(here, count)
            self.own[pl.ds(pl.multiple_of(self.first + self.base + here, 16), count)] = value

        rows_of(part, keep)
        self.base = pl.multiple_of(self.base + begin, 16)
        self.size = part
        self.regions.append((self.base, part))
        self.waiting = sends

    def settle(self):
        self.arrived()
        core = self.place.at["c"]

        def work(row, count):
            here = pl.multiple_of(self.first + self.base + row, 16)
            value = self.total(row, count)
            self.full[core, pl.ds(here, count)] = (value * jnp.abs(value)).astype(BF)

        rows_of(self.size, work)
        self.waiting = []
        self.step()

    def gather(self, group):
        self.arrived()
        core = self.place.at["c"]
        base, size = self.regions.pop()
        ref = self.full.at[core, pl.ds(pl.multiple_of(self.first + base, 16), size)]
        self.waiting = [
            (self.transfers.send(ref, ref, self.place.peer(group, distance)), None, None)
            for distance in range(1, self.plan.count(group))
        ]

    def gather_core(self):
        self.arrived()
        core = self.place.at["c"]
        ref = self.full.at[core, pl.ds(self.first, self.length)]
        self.waiting = [(self.transfers.send(ref, ref, self.place.peer("c", 1)), None, None)]


class Tiny:
    def __init__(self, plan, place, transfers, rows, slots, update):
        self.plan, self.place, self.transfers = plan, place, transfers
        self.rows, self.slots = rows, slots
        self.first, self.size, self.waiting = 0, 0, []
        self.todo = [functools.partial(self.share, dim) for dim in "cxba"] + [self.total, update]
        self.ready = False

    def step(self):
        if self.ready and self.todo:
            self.todo.pop(0)()

    def total(self):
        for copy in self.waiting:
            copy.wait()
        if self.waiting:
            self.rows[...] = sum(self.slots[self.first + index] for index in range(self.size))

    def share(self, dim):
        self.total()
        self.first += self.size
        self.size = self.plan.size[dim]
        slot = self.first + self.place.at[dim]
        self.slots[slot] = self.rows[...]
        ref = self.slots.at[slot]
        self.waiting = [
            self.transfers.send(ref, ref, self.place.peer(dim, distance))
            for distance in range(1, self.size)
        ]


def dot(a, b, dims=((1,), (0,))):
    return lax.dot_general(a, b, (dims, ((), ())), preferred_element_type=F32)


NT = ((1,), (1,))
TN = ((0,), (0,))


def shifted(value, period):
    place = lax.rem(lax.broadcasted_iota(jnp.int32, value.shape, 0), period)
    count = value.shape[0]
    on = jnp.where(place == 0, 0.0, pltpu.roll(value, 1, 0)).astype(BF)
    back = jnp.where(place == period - 1, 0.0, pltpu.roll(value, count - 1, 0)).astype(BF)
    return on, back


def level(feat_r, head_t, head_bias, target, weight, norm):
    pred = dot(head_t, feat_r, NT) + head_bias
    diff = pred - target
    size = jnp.abs(diff)
    loss = weight * jnp.where(size < BETA, 0.5 * diff * diff / BETA, size - 0.5 * BETA) / norm
    dpred = (weight * jnp.clip(diff / BETA, -1.0, 1.0) / norm).astype(BF)
    return loss, dpred


ARGS = (
    ("feats2", "feats3", "match2", "target2", "match3", "target3", "positives", "step_count"),
    ("lat2_w", "lat2_m", "lat2_v", "lat3_w", "lat3_m", "lat3_v", "conv_w", "conv_m", "conv_v"),
    ("head_w", "head_m", "head_v", "bias_w", "bias_m", "bias_v"),
)
RESULTS = (
    ("loss", "w2", "m2", "v2", "c2", "w3", "m3", "v3", "c3", "wc", "mc", "vc", "cc"),
    ("wh", "mh", "vh", "ch", "wb", "mb", "vb", "cb"),
)
SCRATCH = (
    ("own", "send0", "recv0", "send", "recv", "full", "tin", "slots"),
    ("f3", "top_s", "top_p", "strips", "x3", "d3", "k3", "t3", "q3", "tp3", "dtop_s"),
    ("f2", "up", "x2", "d2", "p2", "k2", "t2", "q2", "tt", "ww", "edge_o", "edge_i"),
    ("tl", "wl", "dpl", "lossl", "ps", "dup_f", "dup_s", "dup_r", "dm"),
    ("hp", "ht", "w2b", "local_sem", "out_sem", "in_sem"),
)


class Refs:
    def __init__(self, groups, refs):
        names = [name for group in groups for name in group]
        self.__dict__.update(zip(names, refs, strict=True))


def adamw(weight, first, second, grad, square, scale1, scale2):
    first_new = 0.9 * first + 0.1 * grad
    second_new = 0.95 * second + 0.05 * square
    weight_new = weight - 0.02 * (
        first_new * scale1 / (jnp.sqrt(second_new * scale2) + 1e-08) + 0.1 * weight
    )
    return weight_new, first_new, second_new


def main_kernel(plan, *refs):
    g = Refs(ARGS + RESULTS + SCRATCH, refs)
    place = Place(plan)
    me = place.row
    C, L = plan.width, plan.lanes
    images, rows, cols = plan.images, plan.rows, plan.cols
    H3, W3, strip = plan.high3, plan.cols3, plan.strip
    nrow = plan.nrow

    barrier = pltpu.get_barrier_semaphore()
    greeted = 0
    for distance in range(1, nrow):
        pl.semaphore_signal(
            barrier, inc=1, device_id=(place.img, place.in_row(distance)), device_id_type=MESH
        )
        greeted += 1
    for dim in "cx":
        for distance in range(1, plan.size[dim]):
            pl.semaphore_signal(
                barrier, inc=1, device_id=place.peer(dim, distance), device_id_type=MESH
            )
            greeted += 1

    for group in sorted({group for _, order in plan.jobs for group in order if len(group) > 1}):
        for distance in range(1, plan.count(group)):
            if plan.crosses(group, distance):
                pl.semaphore_signal(
                    barrier, inc=1, device_id=place.peer(group, distance), device_id_type=MESH
                )
                greeted += 1

    transfers = Transfers(g.local_sem, g.out_sem, g.in_sem)
    load = transfers.load
    load_f3 = load(g.feats3, g.f3)
    load_w3 = load(g.lat3_w, g.w3)
    load_bias = load(g.bias_w, g.wb)
    load_head = load(g.head_w, g.wh)
    load_t3 = [load(g.target3.at[0], g.t3), load(g.match3.at[0], g.q3)]

    norm = g.positives[0].astype(F32)
    count = jnp.full((1, LANES), g.step_count[0].astype(F32))
    scale1 = (1.0 / (1.0 - jnp.exp(count * jnp.log(jnp.float32(0.9)))))[:, 0:1]
    scale2 = (1.0 / (1.0 - jnp.exp(count * jnp.log(jnp.float32(0.95)))))[:, 0:1]

    g.top_s[:, 0:8] = jnp.zeros((2, 8, LANES), F32)
    g.top_s[:, 8 + plan.cells3 : 16 + plan.cells3] = jnp.zeros((2, 8, LANES), F32)
    for ref in (g.x3, g.d3):
        ref[0] = jnp.zeros((H3, 3 * C), BF)
        ref[W3 + 1] = jnp.zeros((H3, 3 * C), BF)
    g.hp[...] = jnp.zeros(g.hp.shape, F32)
    for job, (taps, _) in enumerate(plan.jobs):
        used = len(taps) * TAP
        spare = plan.length[job] - used
        if spare:
            at = pl.ds(plan.start[job] + used, spare)
            g.own[at] = jnp.zeros((spare, LANES), F32)
            g.send0[at] = jnp.zeros((spare, LANES), BF)

    load_f3.wait()
    load_w3.wait()
    load_bias.wait()
    load_c3 = load(g.conv_w.at[1], g.wc.at[1])
    load_f2 = [load(g.feats2.at[:, f], g.f2.at[2 + f]) for f in range(rows)]
    load_w2 = load(g.lat2_w, g.w2)
    load_t2 = [load(g.target2, g.t2), load(g.match2, g.q2)]
    load_c2 = load(g.conv_w.at[0], g.wc.at[0])
    top = dot(g.f3[...], g.w3[...].astype(BF)) + g.wb[1:2]
    top = top.astype(BF).astype(F32)
    for half in range(2):
        g.top_s[half, 8 : 8 + plan.cells3] = top[:, half * LANES : (half + 1) * LANES]
    for half in range(2):
        g.top_p[:, half * LANES : (half + 1) * LANES] = g.top_s[half].astype(BF)
    pl.semaphore_wait(barrier, greeted)
    span = (strip + 2) * W3
    strip_sends = []
    for distance in range(1, nrow):
        other = place.in_row(distance)
        src = g.top_p.at[pl.ds(pl.multiple_of(other * strip * W3, 16), span)]
        strip_sends.append(transfers.send(src, g.strips.at[me], (place.img, other)))
    g.strips[me] = g.top_p[pl.ds(pl.multiple_of(me * strip * W3, 16), span)]

    has_up, has_down = me > 0, me < nrow - 1
    up_dev, down_dev = (place.img, me - 1), (place.img, me + 1)
    edge_f2 = []
    for f in range(2):
        edge_f2.append(
            transfers.send(g.feats2.at[:, f], g.f2.at[rows + 2 + f], up_dev, has_up, has_down)
        )
    for f in range(2):
        edge_f2.append(
            transfers.send(g.feats2.at[:, rows - 2 + f], g.f2.at[f], down_dev, has_down, has_up)
        )


    value = jnp.concatenate(
        [
            jnp.concatenate(
                [g.top_s[half, pl.ds(8 + col, H3, stride=W3), :] for half in range(2)], axis=1
            )
            for col in range(W3)
        ],
        axis=0,
    )

    def three(ref, low, middle, high):
        for at, value in enumerate((low, middle, high)):
            ref[1 : W3 + 1, :, at * C : (at + 1) * C] = value.reshape(W3, H3, C)

    on, back = shifted(value, H3)
    three(g.x3, on, value.astype(BF), back)
    load_c3.wait()
    for dx in range(3):
        for dy in range(3):
            tap = dy * 3 + dx
            g.k3[dx, dy * C : (dy + 1) * C] = g.wc[1, tap * C : (tap + 1) * C].astype(BF)
    load_head.wait()
    g.hp[0:12, 0 : C + 1] = g.wh[...]
    g.ht[...] = g.hp[:, 0:C].astype(BF)
    head_bias = g.hp[:, C : C + 1]
    head_t = g.ht[...]

    for copy in load_t3:
        copy.wait()
    g.tp3[...] = jnp.zeros(g.tp3.shape, F32)
    for k in range(12):
        g.tp3[0, k * W3 : (k + 1) * W3, 0:H3] = g.t3[k]
        g.tp3[1, k * W3 : (k + 1) * W3, 0:H3] = g.q3[k // 4].astype(F32)

    def coarse_rows(which):
        return jnp.concatenate(
            [g.tp3[which, pl.ds(col, 16, stride=W3), :][:, 0:H3] for col in range(W3)], axis=1
        )

    target3, weight3 = coarse_rows(0), coarse_rows(1)

    def window3(ref, dx):
        return ref[dx : dx + W3].reshape(plan.cells3, 3 * C)

    coarse = g.wb[3:4] + dot(
        jnp.concatenate([window3(g.x3, dx) for dx in range(3)], axis=1),
        g.k3[...].reshape(9 * C, C),
    )
    coarse_r = coarse.astype(BF)
    loss3, dpred3 = level(coarse_r, head_t, head_bias, target3, weight3, norm)
    head_g = dot(dpred3, coarse_r)
    hbias_g = jnp.sum(dpred3.astype(F32), axis=1, keepdims=True)
    loss = jnp.sum(loss3, axis=1, keepdims=True)
    dcoarse_r = dot(dpred3, head_t, TN).astype(BF)
    out_g3 = jnp.sum(dcoarse_r.astype(F32), axis=0, keepdims=True)
    g.tin[0:16] = head_g
    g.tin[19:20] = out_g3
    on, back = shifted(dcoarse_r.astype(F32), H3)
    three(g.d3, back, dcoarse_r, on)
    core = place.at["c"]

    arrays = {0: (g.wc, g.mc, g.vc, g.cc, 1), 9: (g.wc, g.mc, g.vc, g.cc, 0)}
    arrays |= {18: (g.w2, g.m2, g.v2, g.c2, None), 19: (g.w3, g.m3, g.v3, g.c3, None)}

    def update(taps):
        runs = []
        for tap in taps:
            first = max(start for start in arrays if start <= tap)
            if runs and runs[-1][0] == first:
                runs[-1][2] += TAP
            else:
                runs.append([first, tap, TAP])
        for first, tap, length in runs:
            *held, lead = arrays[first]

            def block(index, carry, first=first, tap=tap, held=held, lead=lead):
                row = pl.multiple_of(plan.tap_row[tap] + index * BLOCK, BLOCK)
                at = pl.ds(pl.multiple_of((tap - first) * TAP + index * BLOCK, BLOCK), BLOCK)
                for half in range(2):
                    lanes = slice(half * LANES, (half + 1) * LANES)
                    where = (at, lanes) if lead is None else (lead, at, lanes)
                    signed = g.full[half, pl.ds(row, BLOCK)].astype(F32)
                    square = jnp.abs(signed)
                    grad = signed * lax.rsqrt(jnp.maximum(square, 1e-37))
                    old = [ref[where] for ref in held[:3]]
                    new = adamw(*old, grad, square, scale1, scale2)
                    for ref, value in zip(held, new):
                        ref[where] = value
                    held[3][where] = new[0].astype(BF)
                return carry

            lax.fori_loop(0, length // BLOCK, block, 0)

    bufs = (g.own, g.send0, g.recv0, g.send, g.recv, g.full)
    jobs = [
        Job(plan, place, number, transfers, bufs, update) for number in range(len(plan.jobs))
    ]

    lane = lax.broadcasted_iota(jnp.int32, (16, LANES), 1)
    diagonal = lane == lax.broadcasted_iota(jnp.int32, (16, LANES), 0)

    def update_tiny():
        hbias = jnp.sum(
            jnp.where(diagonal, jnp.broadcast_to(g.tin[20:21, 0:LANES], (16, LANES)), 0.0),
            axis=1,
            keepdims=True,
        )
        grad = jnp.concatenate([g.tin[0:12], hbias[0:12]], axis=1)
        new = adamw(g.wh[...], g.mh[...], g.vh[...], grad, grad * grad, scale1, scale2)
        for ref, value in zip((g.wh, g.mh, g.vh), new):
            ref[...] = value
        g.ch[...] = new[0].astype(BF)
        grad = g.tin[16:20]
        new = adamw(g.wb[...], g.mb[...], g.vb[...], grad, grad * grad, scale1, scale2)
        for ref, value in zip((g.wb, g.mb, g.vb), new):
            ref[...] = value
        g.cb[...] = new[0].astype(BF)
        g.loss[...] = g.tin[16:24, LANES:]

    small = Tiny(plan, place, transfers, g.tin, g.slots, update_tiny)

    def progress(point):
        for name in SCHEDULE[point]:
            if name == "t":
                small.step()
            elif int(name) < len(jobs):
                jobs[int(name)].step()

    def store_tap(tap, value):
        at = pl.ds(plan.tap_row[tap], TAP)
        left, right = value[:, 0:LANES], value[:, LANES:]
        mine = core == 0
        g.own[at] = jnp.where(mine, left, right)
        g.send0[at] = jnp.where(mine, right, left).astype(BF)
        jobs[plan.tap_job[tap]].stored(tap)

    for dx in range(3):
        grad = dot(window3(g.x3, dx), dcoarse_r, TN)
        for dy in range(3):
            store_tap(dy * 3 + dx, grad[dy * C : (dy + 1) * C])

    dtop = sum(
        dot(window3(g.d3, 2 - dx)[:, dy * C : (dy + 1) * C], g.k3[dx, dy * C : (dy + 1) * C], NT)
        for dx in range(3)
        for dy in range(3)
    )
    for col in range(W3):
        for half in range(2):
            g.dtop_s[half, pl.ds(col, H3, stride=W3), :] = dtop[
                col * H3 : (col + 1) * H3, half * LANES : (half + 1) * LANES
            ]

    late = [
        load(src, dst)
        for src, dst in (
            (g.lat2_m, g.m2),
            (g.lat2_v, g.v2),
            (g.lat3_m, g.m3),
            (g.lat3_v, g.v3),
            (g.conv_m, g.mc),
            (g.conv_v, g.vc),
            (g.head_m, g.mh),
            (g.head_v, g.vh),
            (g.bias_m, g.mb),
            (g.bias_v, g.vb),
        )
    ]

    progress("dtop3")

    for copy in load_t2:
        copy.wait()
    per = LANES // cols
    for part in range(L // LANES):
        g.tt[part] = jnp.zeros(g.tt.shape[1:], F32)
        g.ww[part] = jnp.zeros(g.ww.shape[1:], F32)
        for k in range(12):
            g.tt[part, k * rows : (k + 1) * rows] = jnp.concatenate(
                [g.t2[part * per + n, k] for n in range(per)], axis=1
            )
        for anchor in range(3):
            value = jnp.concatenate(
                [g.q2[part * per + n, anchor] for n in range(per)], axis=1
            ).astype(F32)
            for k in range(anchor * 4, anchor * 4 + 4):
                g.ww[part, k * rows : (k + 1) * rows] = value
        lanes = slice(part * LANES, (part + 1) * LANES)
        for f in range(rows):
            at = pl.ds(f, 16, stride=rows)
            g.tl[1 + f, :, lanes] = g.tt[part, at, :]
            g.wl[1 + f, :, lanes] = g.ww[part, at, :]
    g.edge_o[0, 0:16] = g.tl[1]
    g.edge_o[0, 16:32] = g.wl[1]
    g.edge_o[1, 0:16] = g.tl[rows]
    g.edge_o[1, 16:32] = g.wl[rows]

    edge_up = transfers.send(g.edge_o.at[0], g.edge_i.at[0], up_dev, has_up, has_down)
    edge_down = transfers.send(g.edge_o.at[1], g.edge_i.at[1], down_dev, has_down, has_up)
    progress("target")

    load_w2.wait()
    g.w2b[...] = g.w2[...].astype(BF)
    load_c2.wait()

    g.k2[...] = g.wc[0].astype(BF)

    for copy in load_f2:
        copy.wait()
    for copy in strip_sends:
        copy.wait()
    progress("strips")
    place_i = lax.broadcasted_iota(jnp.int32, ((strip + 2) * cols, span), 0)
    place_j = lax.broadcasted_iota(jnp.int32, ((strip + 2) * cols, span), 1)
    double = jnp.where(place_i // (cols // W3) == place_j, 1.0, 0.0).astype(BF)

    for n in range(images):
        value = dot(double, g.strips[n])
        for cr in range(strip + 2):
            g.up[cr, n] = value[cr * cols : (cr + 1) * cols]
    progress("enlarged")

    def merge(first, count, outside):
        lateral = dot(g.f2[first : first + count].reshape(count * L, C), g.w2b[...]) + g.wb[0:1]
        value = lateral + jnp.concatenate(
            [g.up[j // 2].reshape(L, C) for j in range(first, first + count)], axis=0
        )
        if outside is not None:
            value = jnp.where(outside, 0.0, value)
        value = value.astype(BF)
        on, back = shifted(value.astype(F32), cols)
        for at, part in enumerate((on, value, back)):
            g.x2[first : first + count, :, at * C : (at + 1) * C] = part.reshape(count, L, C)

    def forward(spans):
        lines = [j for first, count in spans for j in range(first, first + count)]
        cells = len(lines) * L
        fine = g.wb[2:3] + dot(
            jnp.concatenate(
                [
                    jnp.concatenate(
                        [g.x2[first + dy : first + dy + count] for first, count in spans], axis=0
                    ).reshape(cells, 3 * C)
                    for dy in range(3)
                ],
                axis=1,
            ),
            g.k2[...],
        )
        fine_r = fine.astype(BF)
        target = jnp.concatenate([g.tl[j] for j in lines], axis=1)
        weight = jnp.concatenate([g.wl[j] for j in lines], axis=1)
        loss2, dpred = level(fine_r, head_t, head_bias, target, weight, norm)
        value = dot(dpred, head_t, TN).astype(BF)
        on, back = shifted(value.astype(F32), cols)
        for at, j in enumerate(lines):
            here = slice(at * L, (at + 1) * L)
            g.p2[j] = fine_r[here]
            g.lossl[j] = loss2[:, here]
            g.dpl[j] = dpred[:, here]
            for side, part in enumerate((back, value, on)):
                g.d2[j, :, side * C : (side + 1) * C] = part[here]

    merge(2, rows, None)
    progress("merged")
    forward([(2, rows - 2)])
    progress("inner")
    for copy in edge_f2 + [edge_up, edge_down]:
        copy.wait()

    @pl.when(has_up)
    def _():
        g.tl[0] = g.edge_i[1, 0:16]
        g.wl[0] = g.edge_i[1, 16:32]

    @pl.when(me == 0)
    def _():
        g.f2[0:2] = jnp.zeros((2, images, cols, C), BF)
        g.tl[0] = jnp.zeros((16, L), F32)
        g.wl[0] = jnp.zeros((16, L), F32)

    @pl.when(has_down)
    def _():
        g.tl[rows + 1] = g.edge_i[0, 0:16]
        g.wl[rows + 1] = g.edge_i[0, 16:32]

    @pl.when(me == nrow - 1)
    def _():
        g.f2[rows + 2 : rows + 4] = jnp.zeros((2, images, cols, C), BF)
        g.tl[rows + 1] = jnp.zeros((16, L), F32)
        g.wl[rows + 1] = jnp.zeros((16, L), F32)


    merge(0, 2, me == 0)
    merge(rows + 2, 2, me == nrow - 1)
    forward([(0, 2), (rows, 2)])
    progress("forward")

    total = sum(
        dot(
            g.d2[2 - dy : 2 - dy + rows].reshape(rows * L, 3 * C)[:, dx * C : (dx + 1) * C],
            g.k2[(dy * 3 + dx) * C : (dy * 3 + dx + 1) * C],
            NT,
        )
        for dy in range(3)
        for dx in range(3)
    )
    g.dm[...] = total.astype(BF).reshape(rows, L, C)
    for q in range(strip):
        pair = total[2 * q * L : (2 * q + 1) * L] + total[(2 * q + 1) * L : (2 * q + 2) * L]
        for half in range(2):
            g.ps[q, half] = pair[:, half * LANES : (half + 1) * LANES]
            value = (
                g.ps[q, half, pl.ds(0, L // 2, stride=2), :]
                + g.ps[q, half, pl.ds(1, L // 2, stride=2), :]
            )
            g.dup_f[:, q * W3 : (q + 1) * W3, half * LANES : (half + 1) * LANES] = value.reshape(
                images, W3, LANES
            )
    g.dup_s[...] = g.dup_f[...].astype(BF)
    dup_sends = []
    for distance in range(1, nrow):
        other = place.in_row(distance)
        dup_sends.append(transfers.send(g.dup_s.at[other], g.dup_r.at[me], (place.img, other)))
    g.dup_r[me] = g.dup_s[me]
    progress("backward")

    inner = g.d2[1 : rows + 1][:, :, C : 2 * C].reshape(rows * L, C)
    for dy in range(3):
        grad = dot(g.x2[dy + 1 : dy + 1 + rows].reshape(rows * L, 3 * C), inner, TN)
        for dx in range(3):
            store_tap(9 + dy * 3 + dx, grad[dx * C : (dx + 1) * C])
        progress(("conv2a", "conv2b", "conv2")[dy])

    dpred2 = jnp.concatenate([g.dpl[1 + f] for f in range(rows)], axis=1)
    g.tin[0:16] += dot(dpred2, g.p2[1 : rows + 1].reshape(rows * L, C))
    hbias_g += jnp.sum(dpred2.astype(F32), axis=1, keepdims=True)
    loss += jnp.sum(sum(g.lossl[1 + f] for f in range(rows)), axis=1, keepdims=True)
    g.tin[20:21, 0:LANES] = jnp.sum(jnp.where(diagonal, hbias_g, 0.0), axis=0, keepdims=True)
    g.tin[20:21, LANES:] = jnp.sum(
        jnp.broadcast_to(loss, (16, LANES)), axis=0, keepdims=True
    )
    g.tin[18:19] = jnp.sum(inner.astype(F32), axis=0, keepdims=True)
    g.tin[21:24] = jnp.zeros((3, C), F32)
    dm = g.dm[...].reshape(rows * L, C)
    store_tap(18, dot(g.f2[2 : rows + 2].reshape(rows * L, C), dm, TN))
    g.tin[16:17] = jnp.sum(dm.astype(F32), axis=0, keepdims=True)
    progress("lat2")

    for copy in dup_sends:
        copy.wait()
    dup = g.dup_r[...].reshape(plan.cells3, C).astype(F32)
    dtop = jnp.concatenate([g.dtop_s[0], g.dtop_s[1]], axis=1) + dup
    dtop_r = dtop.astype(BF)
    lat3_g = dot(g.f3[...], dtop_r, TN)
    store_tap(19, lat3_g[0:TAP])
    store_tap(20, lat3_g[TAP:])
    g.tin[17:18] = jnp.sum(dtop_r.astype(F32), axis=0, keepdims=True)
    small.ready = True
    for copy in late:
        copy.wait()
    progress("lat3")

    while any(job.todo for job in jobs + [small]):
        small.step()
        for job in jobs:
            job.step()
    transfers.close()


def write_kernel(*refs):
    ins, outs, sem = refs[:21], refs[21:42], refs[42]
    copies = []
    for index in range(1, 21):
        src, dst = ins[index], outs[index]
        pairs = [(src, dst)]
        if len(src.shape) == 3:
            pairs = [(src.at[level], dst.at[level]) for level in range(src.shape[0])]
        for pair in pairs:
            copies.append(pltpu.make_async_copy(*pair, sem.at[len(copies)]))
            copies[-1].start()
    outs[0][0] = jnp.max(ins[0][4:5])
    for copy in copies:
        copy.wait()


def body(
    mesh_shape,
    feats2,
    feats3,
    match2,
    target2,
    match3,
    target3,
    positives,
    step_count,
    lat2_w,
    lat2_m,
    lat2_v,
    lat3_w,
    lat3_m,
    lat3_v,
    conv_w,
    conv_m,
    conv_v,
    head_w,
    head_m,
    head_v,
    bias_w,
    bias_m,
    bias_v,
):
    plan = Plan(mesh_shape, feats2.shape, feats3.shape)
    C, L, H3, W3 = plan.width, plan.lanes, plan.high3, plan.cols3
    images, rows, cols, strip, nrow = plan.images, plan.rows, plan.cols, plan.strip, plan.nrow
    head = [x.T for x in (head_w, head_m, head_v)]
    weights = [lat2_w, lat2_m, lat2_v, lat3_w, lat3_m, lat3_v, conv_w, conv_m, conv_v]
    weights += head + [bias_w, bias_m, bias_v]
    args = [
        feats2,
        feats3.reshape(plan.cells3, plan.width3),
        match2,
        target2,
        match3.transpose(0, 1, 3, 2),
        target3.transpose(0, 1, 3, 2),
    ]
    args = [pltpu.with_memory_space_constraint(x, HBM) for x in args]
    held = [pltpu.with_memory_space_constraint(x, HBM) for x in weights]
    hbm, vmem, smem = (pl.BlockSpec(memory_space=space) for space in (HBM, VMEM, SMEM))
    outs = [VMEM((8, LANES), F32)]
    for x in (lat2_w, lat3_w, conv_w, head[0], bias_w):
        outs += [VMEM(x.shape, F32)] * 3 + [VMEM(x.shape, BF)]
    span = (strip + 2) * W3
    dma = pltpu.SemaphoreType.DMA
    remotes = 2 * (nrow - 1) + 6 + plan.tiny_links + len(plan.jobs) * 2 * plan.links
    scratch = [
        VMEM((plan.total, LANES), F32),
        VMEM((plan.total, LANES), BF),
        VMEM((plan.total, LANES), BF),
        VMEM((plan.total, LANES), BF),
        VMEM((plan.total, LANES), BF),
        VMEM((2, plan.total, LANES), BF),
        VMEM((TINY, C), F32),
        VMEM((sum(plan.size.values()), TINY, C), F32),
        VMEM((plan.cells3, plan.width3), BF),
        VMEM((2, plan.cells3 + 16, LANES), F32),
        VMEM((plan.cells3 + 16, C), BF),
        VMEM((nrow, span, C), BF),
        VMEM((W3 + 2, H3, 3 * C), BF),
        VMEM((W3 + 2, H3, 3 * C), BF),
        VMEM((3, 3 * C, C), BF),
        VMEM((12, W3, H3), F32),
        VMEM((3, W3, H3), jnp.int32),
        VMEM((2, 16 * W3, LANES), F32),
        VMEM((2, plan.cells3, LANES), F32),
        VMEM((rows + 4, images, cols, C), BF),
        VMEM((strip + 2, images, cols, C), F32),
        VMEM((rows + 4, L, 3 * C), BF),
        VMEM((rows + 2, L, 3 * C), BF),
        VMEM((rows + 2, L, C), BF),
        VMEM((9 * C, C), BF),
        VMEM(target2.shape, F32),
        VMEM(match2.shape, jnp.int32),
        VMEM((L // LANES, 16 * rows, LANES), F32),
        VMEM((L // LANES, 16 * rows, LANES), F32),
        VMEM((2, 32, L), F32),
        VMEM((2, 32, L), F32),
        VMEM((rows + 2, 16, L), F32),
        VMEM((rows + 2, 16, L), F32),
        VMEM((rows + 2, 16, L), BF),
        VMEM((rows + 2, 16, L), F32),
        VMEM((strip, 2, L, LANES), F32),
        VMEM((images, strip * W3, C), F32),
        VMEM((images, strip * W3, C), BF),
        VMEM((nrow, strip * W3, C), BF),
        VMEM((rows, L, C), BF),
        VMEM((16, 3 * LANES), F32),
        VMEM((16, C), BF),
        VMEM((C, C), BF),
        dma((48,)),
        dma((remotes,)),
        dma((remotes,)),
    ]
    results = pl.pallas_call(
        functools.partial(main_kernel, plan),
        out_shape=outs,
        in_specs=[hbm] * 6 + [smem] * 2 + [hbm] * len(held),
        out_specs=[vmem] * len(outs),
        scratch_shapes=scratch,
        compiler_params=pltpu.CompilerParams(
            collective_id=0, has_side_effects=True, vmem_limit_bytes=40 << 20
        ),
        name="gradients",
    )(*args, positives.reshape(1), step_count.reshape(1), *held)
    kept = [pltpu.with_memory_space_constraint(x, VMEM) for x in results]

    shapes = [jax.ShapeDtypeStruct((1,), F32)]
    shapes += [jax.ShapeDtypeStruct(x.shape, x.dtype) for x in kept[1:]]
    new = pl.pallas_call(
        write_kernel,
        out_shape=shapes,
        in_specs=[vmem] * len(kept),
        out_specs=[smem] + [hbm] * 20,
        scratch_shapes=[dma((24,))],
        compiler_params=pltpu.CompilerParams(vmem_limit_bytes=1 << 20),
        name="results",
    )(*kept)
    outs = [new[0].reshape(())] + list(new[1:])
    for index in range(13, 17):
        outs[index] = outs[index].T
    return tuple(outs)


def solution(mesh):
    split = (
        P("img", "row", None, None),
        P(("img", "row"), None, None, None),
        P("img", None, "row", None),
        P("img", None, "row", None),
        P(("img", "row"), None, None, None),
        P(("img", "row"), None, None, None),
    )
    return jax.shard_map(
        functools.partial(body, dict(mesh.shape)),
        mesh=mesh,
        in_specs=split + (P(),) * 17,
        out_specs=(P(),) * 21,
        check_vma=False,
    )
```

```python
import functools

import jax
import jax.numpy as jnp
from jax import lax
from jax.experimental import pallas as pl
from jax.experimental.pallas import tpu as pltpu
from jax.sharding import PartitionSpec as P

BETA = 1.0 / 9.0
MESH = pl.DeviceIdType.MESH
VMEM = pltpu.MemorySpace.VMEM
SMEM = pltpu.MemorySpace.SMEM
HBM = pltpu.MemorySpace.HBM
BF = jnp.bfloat16
F32 = jnp.float32
LANES = 128
TAP = 256
BLOCK = 256
TAPS = 21
FINE_JOBS = (
    (range(0, 5), ("xb", "a")),
    (range(5, 9), ("xb", "a")),
    (range(9, 12), ("xb", "a")),
    (range(12, 15), ("xb", "a")),
    (range(15, 19), ("xb", "a")),
    (range(19, 21), ("xb", "a")),
)
SCHEDULE = {'dtop3': '', 'target': '01', 'strips': '', 'enlarged': '', 'merged': '', 'inner': '', 'forward': '', 'backward': '23', 'conv2a': '', 'conv2b': '', 'conv2': '0', 'lat2': '14', 'lat3': 'tt5021t34t02513tt420530145212334545'}
LARGE_JOBS = (
    (range(0, 8), ("x", "b", "a")),
    (range(8, 16), ("b", "x", "a")),
    (range(16, 21), ("x", "b", "a")),
)
TINY = 24


class Plan:
    def __init__(self, mesh_shape, feats2, feats3):
        self.nimg, self.nrow = mesh_shape["img"], mesh_shape["row"]
        self.images, self.rows, self.cols, self.width = feats2
        self.high3, self.cols3, self.width3 = feats3[1:]
        self.strip = self.high3 // self.nrow
        self.lanes = self.images * self.cols
        self.cells3 = self.high3 * self.cols3
        minor = 1
        while minor * minor * 4 <= self.nrow:
            minor *= 2
        self.size = {"c": 2, "x": self.nimg // 2, "b": minor, "a": self.nrow // minor}
        grain = 16 * self.size["x"] * self.nrow
        self.jobs = FINE_JOBS if grain <= TAP else LARGE_JOBS
        self.start, self.length, self.tap_row, self.tap_job = [], [], {}, {}
        row = 0
        for number, (taps, _) in enumerate(self.jobs):
            self.start.append(row)
            for place, tap in enumerate(taps):
                self.tap_row[tap] = row + place * TAP
                self.tap_job[tap] = number
            self.length.append(-(-len(taps) * TAP // grain) * grain)
            row += self.length[-1]
        self.total = row
        self.tiny_links = sum(self.size.values()) - 4
        self.links = 1 + max(
            sum(self.count(group) - 1 for group in order) for _, order in self.jobs
        )

    def count(self, group):
        number = 1
        for dim in group:
            number *= self.size[dim]
        return number

    def crosses(self, group, distance):
        moved = set()
        for dim in group[::-1]:
            step, distance = distance % self.size[dim], distance // self.size[dim]
            if step:
                moved.add(dim)
        return "x" in moved and len(moved) > 1


class Place:
    def __init__(self, plan):
        self.plan = plan
        self.img, self.row = lax.axis_index("img"), lax.axis_index("row")
        minor = plan.size["b"]
        self.at = {
            "c": lax.rem(self.img, 2),
            "x": self.img // 2,
            "b": lax.rem(self.row, minor),
            "a": self.row // minor,
        }

    def moved(self, group, distance):
        at = dict(self.at)
        for dim in group[::-1]:
            size = self.plan.size[dim]
            step, distance = distance % size, distance // size
            if step:
                at[dim] = lax.rem(at[dim] + step, size)
        return at

    def coord(self, group, distance=0):
        at = self.moved(group, distance)
        number = 0
        for dim in group:
            number = number * self.plan.size[dim] + at[dim]
        return number

    def peer(self, group, distance):
        at = self.moved(group, distance)
        return (at["x"] * 2 + at["c"], at["a"] * self.plan.size["b"] + at["b"])

    def in_row(self, distance):
        return lax.rem(self.row + distance + self.plan.nrow, self.plan.nrow)


def when(condition, work):
    if condition is None:
        work()
    else:
        pl.when(condition)(work)


class Transfer:
    def __init__(self, copy, remote, out_if=None, in_if=None):
        self.copy, self.remote, self.out_if, self.in_if = copy, remote, out_if, in_if
        self.landed = self.left = False
        when(out_if, copy.start)

    def wait(self):
        if not self.landed:
            when(self.in_if, self.copy.wait_recv if self.remote else self.copy.wait)
        self.landed = True

    def close(self):
        self.wait()
        if self.remote and not self.left:
            when(self.out_if, self.copy.wait_send)
        self.left = True


class Transfers:
    def __init__(self, local, out, into):
        self.local, self.out, self.into = local, out, into
        self.all, self.locals, self.remotes = [], 0, 0

    def load(self, src, dst):
        copy = pltpu.make_async_copy(src, dst, self.local.at[self.locals])
        self.locals += 1
        self.all.append(Transfer(copy, False))
        return self.all[-1]

    def send(self, src, dst, peer, out_if=None, in_if=None):
        copy = pltpu.make_async_remote_copy(
            src_ref=src,
            dst_ref=dst,
            send_sem=self.out.at[self.remotes],
            recv_sem=self.into.at[self.remotes],
            device_id=peer,
            device_id_type=MESH,
        )
        self.remotes += 1
        self.all.append(Transfer(copy, True, out_if, in_if))
        return self.all[-1]

    def close(self):
        for transfer in self.all:
            transfer.close()


def rows_of(count, work, block=640):
    if count <= block or count % block:
        work(0, count)
        return

    def step(index, carry):
        work(pl.multiple_of(index * block, block), block)
        return carry

    lax.fori_loop(0, count // block, step, 0)


class Job:
    def __init__(self, plan, place, number, transfers, bufs, update):
        self.plan, self.place, self.number, self.transfers = plan, place, number, transfers
        self.own, self.send0, self.recv0, self.send, self.recv, self.full = bufs
        self.first, self.length = plan.start[number], plan.length[number]
        taps, self.order = plan.jobs[number]
        self.missing = set(taps)
        self.base, self.size = 0, self.length
        self.regions = []
        self.spare = 0
        self.waiting = []
        self.todo = [self.core] + [functools.partial(self.scatter, group) for group in self.order]
        self.todo += [self.settle]
        self.todo += [functools.partial(self.gather, group) for group in self.order[::-1]]
        self.todo += [self.gather_core, functools.partial(self.finish, update, taps)]

    @property
    def ready(self):
        return not self.missing and bool(self.todo)

    def step(self, steps=1):
        for _ in range(steps):
            if self.ready:
                self.todo.pop(0)()

    def stored(self, tap):
        self.missing.remove(tap)
        if not self.missing:
            self.step()

    def core(self):
        rows = pl.ds(self.first, self.length)
        copy = self.transfers.send(
            self.send0.at[rows], self.recv0.at[rows], self.place.peer("c", 1)
        )
        self.waiting = [(copy, self.recv0, self.first)]

    def arrived(self):
        for copy, _, _ in self.waiting:
            copy.wait()

    def finish(self, update, taps):
        self.arrived()
        update(taps)

    def total(self, row, count):
        at = pl.multiple_of(self.first + self.base + row, 16)
        value = self.own[pl.ds(at, count)]
        for _, ref, start in self.waiting:
            value = value + ref[pl.ds(pl.multiple_of(start + row, 16), count)].astype(F32)
        return value

    def scatter(self, group):
        self.arrived()
        size = self.plan.count(group)
        part = self.size // size
        sends = []
        for distance in range(1, size):
            begin = pl.multiple_of(self.place.coord(group, distance) * part, 16)
            spot = self.first + self.spare

            def work(row, count, begin=begin, spot=spot):
                self.send[pl.ds(pl.multiple_of(spot + row, 16), count)] = self.total(
                    pl.multiple_of(begin + row, 16), count
                ).astype(BF)

            rows_of(part, work)
            rows = pl.ds(spot, part)
            copy = self.transfers.send(
                self.send.at[rows], self.recv.at[rows], self.place.peer(group, distance)
            )
            sends.append((copy, self.recv, spot))
            self.spare += part
        begin = pl.multiple_of(self.place.coord(group) * part, 16)

        def keep(row, count):
            here = pl.multiple_of(begin + row, 16)
            value = self.total(here, count)
            self.own[pl.ds(pl.multiple_of(self.first + self.base + here, 16), count)] = value

        rows_of(part, keep)
        self.base = pl.multiple_of(self.base + begin, 16)
        self.size = part
        self.regions.append((self.base, part))
        self.waiting = sends

    def settle(self):
        self.arrived()
        core = self.place.at["c"]

        def work(row, count):
            here = pl.multiple_of(self.first + self.base + row, 16)
            value = self.total(row, count)
            self.full[core, pl.ds(here, count)] = (value * jnp.abs(value)).astype(BF)

        rows_of(self.size, work)
        self.waiting = []
        self.step()

    def gather(self, group):
        self.arrived()
        core = self.place.at["c"]
        base, size = self.regions.pop()
        ref = self.full.at[core, pl.ds(pl.multiple_of(self.first + base, 16), size)]
        self.waiting = [
            (self.transfers.send(ref, ref, self.place.peer(group, distance)), None, None)
            for distance in range(1, self.plan.count(group))
        ]

    def gather_core(self):
        self.arrived()
        core = self.place.at["c"]
        ref = self.full.at[core, pl.ds(self.first, self.length)]
        self.waiting = [(self.transfers.send(ref, ref, self.place.peer("c", 1)), None, None)]


class Tiny:
    def __init__(self, plan, place, transfers, rows, slots, update):
        self.plan, self.place, self.transfers = plan, place, transfers
        self.rows, self.slots = rows, slots
        self.first, self.size, self.waiting = 0, 0, []
        self.todo = [functools.partial(self.share, dim) for dim in "cxba"] + [self.total, update]
        self.ready = False

    def step(self):
        if self.ready and self.todo:
            self.todo.pop(0)()

    def total(self):
        for copy in self.waiting:
            copy.wait()
        if self.waiting:
            self.rows[...] = sum(self.slots[self.first + index] for index in range(self.size))

    def share(self, dim):
        self.total()
        self.first += self.size
        self.size = self.plan.size[dim]
        slot = self.first + self.place.at[dim]
        self.slots[slot] = self.rows[...]
        ref = self.slots.at[slot]
        self.waiting = [
            self.transfers.send(ref, ref, self.place.peer(dim, distance))
            for distance in range(1, self.size)
        ]


def dot(a, b, dims=((1,), (0,))):
    return lax.dot_general(a, b, (dims, ((), ())), preferred_element_type=F32)


NT = ((1,), (1,))
TN = ((0,), (0,))


def shifted(value, period):
    place = lax.rem(lax.broadcasted_iota(jnp.int32, value.shape, 0), period)
    count = value.shape[0]
    on = jnp.where(place == 0, 0.0, pltpu.roll(value, 1, 0)).astype(BF)
    back = jnp.where(place == period - 1, 0.0, pltpu.roll(value, count - 1, 0)).astype(BF)
    return on, back


def level(feat_r, head_t, head_bias, target, weight, norm):
    pred = dot(head_t, feat_r, NT) + head_bias
    diff = pred - target
    size = jnp.abs(diff)
    loss = weight * jnp.where(size < BETA, 0.5 * diff * diff / BETA, size - 0.5 * BETA) / norm
    dpred = (weight * jnp.clip(diff / BETA, -1.0, 1.0) / norm).astype(BF)
    return loss, dpred


ARGS = (
    ("feats2", "feats3", "match2", "target2", "match3", "target3", "positives", "step_count"),
    ("lat2_w", "lat2_m", "lat2_v", "lat3_w", "lat3_m", "lat3_v", "conv_w", "conv_m", "conv_v"),
    ("head_w", "head_m", "head_v", "bias_w", "bias_m", "bias_v"),
)
RESULTS = (
    ("loss", "w2", "m2", "v2", "c2", "w3", "m3", "v3", "c3", "wc", "mc", "vc", "cc"),
    ("wh", "mh", "vh", "ch", "wb", "mb", "vb", "cb"),
)
SCRATCH = (
    ("own", "send0", "recv0", "send", "recv", "full", "tin", "slots"),
    ("f3", "top_s", "top_p", "strips", "x3", "d3", "k3", "t3", "q3", "tp3", "dtop_s"),
    ("f2", "up", "x2", "d2", "p2", "k2", "t2", "q2", "tt", "ww", "edge_o", "edge_i"),
    ("tl", "wl", "dpl", "lossl", "ps", "dup_f", "dup_s", "dup_r", "dm"),
    ("hp", "ht", "w2b", "local_sem", "out_sem", "in_sem"),
)


class Refs:
    def __init__(self, groups, refs):
        names = [name for group in groups for name in group]
        self.__dict__.update(zip(names, refs, strict=True))


def adamw(weight, first, second, grad, square, scale1, scale2):
    first_new = 0.9 * first + 0.1 * grad
    second_new = 0.95 * second + 0.05 * square
    weight_new = weight - 0.02 * (
        first_new * scale1 / (jnp.sqrt(second_new * scale2) + 1e-08) + 0.1 * weight
    )
    return weight_new, first_new, second_new


def main_kernel(plan, *refs):
    g = Refs(ARGS + RESULTS + SCRATCH, refs)
    place = Place(plan)
    me = place.row
    C, L = plan.width, plan.lanes
    images, rows, cols = plan.images, plan.rows, plan.cols
    H3, W3, strip = plan.high3, plan.cols3, plan.strip
    nrow = plan.nrow

    barrier = pltpu.get_barrier_semaphore()
    greeted = 0
    for distance in range(1, nrow):
        pl.semaphore_signal(
            barrier, inc=1, device_id=(place.img, place.in_row(distance)), device_id_type=MESH
        )
        greeted += 1
    for dim in "cx":
        for distance in range(1, plan.size[dim]):
            pl.semaphore_signal(
                barrier, inc=1, device_id=place.peer(dim, distance), device_id_type=MESH
            )
            greeted += 1

    for group in sorted({group for _, order in plan.jobs for group in order if len(group) > 1}):
        for distance in range(1, plan.count(group)):
            if plan.crosses(group, distance):
                pl.semaphore_signal(
                    barrier, inc=1, device_id=place.peer(group, distance), device_id_type=MESH
                )
                greeted += 1

    transfers = Transfers(g.local_sem, g.out_sem, g.in_sem)
    load = transfers.load
    load_f3 = load(g.feats3, g.f3)
    load_w3 = load(g.lat3_w, g.w3)
    load_bias = load(g.bias_w, g.wb)
    load_head = load(g.head_w, g.wh)
    load_t3 = [load(g.target3.at[0], g.t3), load(g.match3.at[0], g.q3)]

    norm = g.positives[0].astype(F32)
    count = jnp.full((1, LANES), g.step_count[0].astype(F32))
    scale1 = (1.0 / (1.0 - jnp.exp(count * jnp.log(jnp.float32(0.9)))))[:, 0:1]
    scale2 = (1.0 / (1.0 - jnp.exp(count * jnp.log(jnp.float32(0.95)))))[:, 0:1]

    g.top_s[:, 0:8] = jnp.zeros((2, 8, LANES), F32)
    g.top_s[:, 8 + plan.cells3 : 16 + plan.cells3] = jnp.zeros((2, 8, LANES), F32)
    for ref in (g.x3, g.d3):
        ref[0] = jnp.zeros((H3, 3 * C), BF)
        ref[W3 + 1] = jnp.zeros((H3, 3 * C), BF)
    g.hp[...] = jnp.zeros(g.hp.shape, F32)
    for job, (taps, _) in enumerate(plan.jobs):
        used = len(taps) * TAP
        spare = plan.length[job] - used
        if spare:
            at = pl.ds(plan.start[job] + used, spare)
            g.own[at] = jnp.zeros((spare, LANES), F32)
            g.send0[at] = jnp.zeros((spare, LANES), BF)

    load_f3.wait()
    load_w3.wait()
    load_bias.wait()
    load_c3 = load(g.conv_w.at[1], g.wc.at[1])
    load_f2 = [load(g.feats2.at[:, f], g.f2.at[2 + f]) for f in range(rows)]
    load_w2 = load(g.lat2_w, g.w2)
    load_t2 = [load(g.target2, g.t2), load(g.match2, g.q2)]
    load_c2 = load(g.conv_w.at[0], g.wc.at[0])
    top = dot(g.f3[...], g.w3[...].astype(BF)) + g.wb[1:2]
    top = top.astype(BF).astype(F32)
    for half in range(2):
        g.top_s[half, 8 : 8 + plan.cells3] = top[:, half * LANES : (half + 1) * LANES]
    for half in range(2):
        g.top_p[:, half * LANES : (half + 1) * LANES] = g.top_s[half].astype(BF)
    pl.semaphore_wait(barrier, greeted)
    span = (strip + 2) * W3
    strip_sends = []
    for distance in range(1, nrow):
        other = place.in_row(distance)
        src = g.top_p.at[pl.ds(pl.multiple_of(other * strip * W3, 16), span)]
        strip_sends.append(transfers.send(src, g.strips.at[me], (place.img, other)))
    g.strips[me] = g.top_p[pl.ds(pl.multiple_of(me * strip * W3, 16), span)]

    has_up, has_down = me > 0, me < nrow - 1
    up_dev, down_dev = (place.img, me - 1), (place.img, me + 1)
    edge_f2 = []
    for f in range(2):
        edge_f2.append(
            transfers.send(g.feats2.at[:, f], g.f2.at[rows + 2 + f], up_dev, has_up, has_down)
        )
    for f in range(2):
        edge_f2.append(
            transfers.send(g.feats2.at[:, rows - 2 + f], g.f2.at[f], down_dev, has_down, has_up)
        )


    value = jnp.concatenate(
        [
            jnp.concatenate(
                [g.top_s[half, pl.ds(8 + col, H3, stride=W3), :] for half in range(2)], axis=1
            )
            for col in range(W3)
        ],
        axis=0,
    )

    def three(ref, low, middle, high):
        for at, value in enumerate((low, middle, high)):
            ref[1 : W3 + 1, :, at * C : (at + 1) * C] = value.reshape(W3, H3, C)

    on, back = shifted(value, H3)
    three(g.x3, on, value.astype(BF), back)
    load_c3.wait()
    for dx in range(3):
        for dy in range(3):
            tap = dy * 3 + dx
            g.k3[dx, dy * C : (dy + 1) * C] = g.wc[1, tap * C : (tap + 1) * C].astype(BF)
    load_head.wait()
    g.hp[0:12, 0 : C + 1] = g.wh[...]
    g.ht[...] = g.hp[:, 0:C].astype(BF)
    head_bias = g.hp[:, C : C + 1]
    head_t = g.ht[...]

    for copy in load_t3:
        copy.wait()
    g.tp3[...] = jnp.zeros(g.tp3.shape, F32)
    for k in range(12):
        g.tp3[0, k * W3 : (k + 1) * W3, 0:H3] = g.t3[k]
        g.tp3[1, k * W3 : (k + 1) * W3, 0:H3] = g.q3[k // 4].astype(F32)

    def coarse_rows(which):
        return jnp.concatenate(
            [g.tp3[which, pl.ds(col, 16, stride=W3), :][:, 0:H3] for col in range(W3)], axis=1
        )

    target3, weight3 = coarse_rows(0), coarse_rows(1)

    def window3(ref, dx):
        return ref[dx : dx + W3].reshape(plan.cells3, 3 * C)

    coarse = g.wb[3:4] + dot(
        jnp.concatenate([window3(g.x3, dx) for dx in range(3)], axis=1),
        g.k3[...].reshape(9 * C, C),
    )
    coarse_r = coarse.astype(BF)
    loss3, dpred3 = level(coarse_r, head_t, head_bias, target3, weight3, norm)
    head_g = dot(dpred3, coarse_r)
    hbias_g = jnp.sum(dpred3.astype(F32), axis=1, keepdims=True)
    loss = jnp.sum(loss3, axis=1, keepdims=True)
    dcoarse_r = dot(dpred3, head_t, TN).astype(BF)
    out_g3 = jnp.sum(dcoarse_r.astype(F32), axis=0, keepdims=True)
    g.tin[0:16] = head_g
    g.tin[19:20] = out_g3
    on, back = shifted(dcoarse_r.astype(F32), H3)
    three(g.d3, back, dcoarse_r, on)
    core = place.at["c"]

    arrays = {0: (g.wc, g.mc, g.vc, g.cc, 1), 9: (g.wc, g.mc, g.vc, g.cc, 0)}
    arrays |= {18: (g.w2, g.m2, g.v2, g.c2, None), 19: (g.w3, g.m3, g.v3, g.c3, None)}

    def update(taps):
        runs = []
        for tap in taps:
            first = max(start for start in arrays if start <= tap)
            if runs and runs[-1][0] == first:
                runs[-1][2] += TAP
            else:
                runs.append([first, tap, TAP])
        for first, tap, length in runs:
            *held, lead = arrays[first]

            def block(index, carry, first=first, tap=tap, held=held, lead=lead):
                row = pl.multiple_of(plan.tap_row[tap] + index * BLOCK, BLOCK)
                at = pl.ds(pl.multiple_of((tap - first) * TAP + index * BLOCK, BLOCK), BLOCK)
                for half in range(2):
                    lanes = slice(half * LANES, (half + 1) * LANES)
                    where = (at, lanes) if lead is None else (lead, at, lanes)
                    signed = g.full[half, pl.ds(row, BLOCK)].astype(F32)
                    square = jnp.abs(signed)
                    grad = signed * lax.rsqrt(jnp.maximum(square, 1e-37))
                    old = [ref[where] for ref in held[:3]]
                    new = adamw(*old, grad, square, scale1, scale2)
                    for ref, value in zip(held, new):
                        ref[where] = value
                    held[3][where] = new[0].astype(BF)
                return carry

            lax.fori_loop(0, length // BLOCK, block, 0)

    bufs = (g.own, g.send0, g.recv0, g.send, g.recv, g.full)
    jobs = [
        Job(plan, place, number, transfers, bufs, update) for number in range(len(plan.jobs))
    ]

    lane = lax.broadcasted_iota(jnp.int32, (16, LANES), 1)
    diagonal = lane == lax.broadcasted_iota(jnp.int32, (16, LANES), 0)

    def update_tiny():
        hbias = jnp.sum(
            jnp.where(diagonal, jnp.broadcast_to(g.tin[20:21, 0:LANES], (16, LANES)), 0.0),
            axis=1,
            keepdims=True,
        )
        grad = jnp.concatenate([g.tin[0:12], hbias[0:12]], axis=1)
        new = adamw(g.wh[...], g.mh[...], g.vh[...], grad, grad * grad, scale1, scale2)
        for ref, value in zip((g.wh, g.mh, g.vh), new):
            ref[...] = value
        g.ch[...] = new[0].astype(BF)
        grad = g.tin[16:20]
        new = adamw(g.wb[...], g.mb[...], g.vb[...], grad, grad * grad, scale1, scale2)
        for ref, value in zip((g.wb, g.mb, g.vb), new):
            ref[...] = value
        g.cb[...] = new[0].astype(BF)
        g.loss[...] = g.tin[16:24, LANES:]

    small = Tiny(plan, place, transfers, g.tin, g.slots, update_tiny)

    def progress(point):
        for name in SCHEDULE[point]:
            if name == "t":
                small.step()
            elif int(name) < len(jobs):
                jobs[int(name)].step()

    def store_tap(tap, value):
        at = pl.ds(plan.tap_row[tap], TAP)
        left, right = value[:, 0:LANES], value[:, LANES:]
        mine = core == 0
        g.own[at] = jnp.where(mine, left, right)
        g.send0[at] = jnp.where(mine, right, left).astype(BF)
        jobs[plan.tap_job[tap]].stored(tap)

    for dx in range(3):
        grad = dot(window3(g.x3, dx), dcoarse_r, TN)
        for dy in range(3):
            store_tap(dy * 3 + dx, grad[dy * C : (dy + 1) * C])

    dtop = sum(
        dot(window3(g.d3, 2 - dx)[:, dy * C : (dy + 1) * C], g.k3[dx, dy * C : (dy + 1) * C], NT)
        for dx in range(3)
        for dy in range(3)
    )
    for col in range(W3):
        for half in range(2):
            g.dtop_s[half, pl.ds(col, H3, stride=W3), :] = dtop[
                col * H3 : (col + 1) * H3, half * LANES : (half + 1) * LANES
            ]

    late = [
        load(src, dst)
        for src, dst in (
            (g.lat2_m, g.m2),
            (g.lat2_v, g.v2),
            (g.lat3_m, g.m3),
            (g.lat3_v, g.v3),
            (g.conv_m, g.mc),
            (g.conv_v, g.vc),
            (g.head_m, g.mh),
            (g.head_v, g.vh),
            (g.bias_m, g.mb),
            (g.bias_v, g.vb),
        )
    ]

    progress("dtop3")

    for copy in load_t2:
        copy.wait()
    per = LANES // cols
    for part in range(L // LANES):
        g.tt[part] = jnp.zeros(g.tt.shape[1:], F32)
        g.ww[part] = jnp.zeros(g.ww.shape[1:], F32)
        for k in range(12):
            g.tt[part, k * rows : (k + 1) * rows] = jnp.concatenate(
                [g.t2[part * per + n, k] for n in range(per)], axis=1
            )
        for anchor in range(3):
            value = jnp.concatenate(
                [g.q2[part * per + n, anchor] for n in range(per)], axis=1
            ).astype(F32)
            for k in range(anchor * 4, anchor * 4 + 4):
                g.ww[part, k * rows : (k + 1) * rows] = value
        lanes = slice(part * LANES, (part + 1) * LANES)
        for f in range(rows):
            at = pl.ds(f, 16, stride=rows)
            g.tl[1 + f, :, lanes] = g.tt[part, at, :]
            g.wl[1 + f, :, lanes] = g.ww[part, at, :]
    g.edge_o[0, 0:16] = g.tl[1]
    g.edge_o[0, 16:32] = g.wl[1]
    g.edge_o[1, 0:16] = g.tl[rows]
    g.edge_o[1, 16:32] = g.wl[rows]

    edge_up = transfers.send(g.edge_o.at[0], g.edge_i.at[0], up_dev, has_up, has_down)
    edge_down = transfers.send(g.edge_o.at[1], g.edge_i.at[1], down_dev, has_down, has_up)
    progress("target")

    load_w2.wait()
    g.w2b[...] = g.w2[...].astype(BF)
    load_c2.wait()

    g.k2[...] = g.wc[0].astype(BF)

    for copy in load_f2:
        copy.wait()
    for copy in strip_sends:
        copy.wait()
    progress("strips")
    place_i = lax.broadcasted_iota(jnp.int32, ((strip + 2) * cols, span), 0)
    place_j = lax.broadcasted_iota(jnp.int32, ((strip + 2) * cols, span), 1)
    double = jnp.where(place_i // (cols // W3) == place_j, 1.0, 0.0).astype(BF)

    for n in range(images):
        value = dot(double, g.strips[n])
        for cr in range(strip + 2):
            g.up[cr, n] = value[cr * cols : (cr + 1) * cols]
    progress("enlarged")

    def merge(first, count, outside):
        lateral = dot(g.f2[first : first + count].reshape(count * L, C), g.w2b[...]) + g.wb[0:1]
        value = lateral + jnp.concatenate(
            [g.up[j // 2].reshape(L, C) for j in range(first, first + count)], axis=0
        )
        if outside is not None:
            value = jnp.where(outside, 0.0, value)
        value = value.astype(BF)
        on, back = shifted(value.astype(F32), cols)
        for at, part in enumerate((on, value, back)):
            g.x2[first : first + count, :, at * C : (at + 1) * C] = part.reshape(count, L, C)

    def forward(spans):
        lines = [j for first, count in spans for j in range(first, first + count)]
        cells = len(lines) * L
        fine = g.wb[2:3] + dot(
            jnp.concatenate(
                [
                    jnp.concatenate(
                        [g.x2[first + dy : first + dy + count] for first, count in spans], axis=0
                    ).reshape(cells, 3 * C)
                    for dy in range(3)
                ],
                axis=1,
            ),
            g.k2[...],
        )
        fine_r = fine.astype(BF)
        target = jnp.concatenate([g.tl[j] for j in lines], axis=1)
        weight = jnp.concatenate([g.wl[j] for j in lines], axis=1)
        loss2, dpred = level(fine_r, head_t, head_bias, target, weight, norm)
        value = dot(dpred, head_t, TN).astype(BF)
        on, back = shifted(value.astype(F32), cols)
        for at, j in enumerate(lines):
            here = slice(at * L, (at + 1) * L)
            g.p2[j] = fine_r[here]
            g.lossl[j] = loss2[:, here]
            g.dpl[j] = dpred[:, here]
            for side, part in enumerate((back, value, on)):
                g.d2[j, :, side * C : (side + 1) * C] = part[here]

    merge(2, rows, None)
    progress("merged")
    forward([(2, rows - 2)])
    progress("inner")
    for copy in edge_f2 + [edge_up, edge_down]:
        copy.wait()

    @pl.when(has_up)
    def _():
        g.tl[0] = g.edge_i[1, 0:16]
        g.wl[0] = g.edge_i[1, 16:32]

    @pl.when(me == 0)
    def _():
        g.f2[0:2] = jnp.zeros((2, images, cols, C), BF)
        g.tl[0] = jnp.zeros((16, L), F32)
        g.wl[0] = jnp.zeros((16, L), F32)

    @pl.when(has_down)
    def _():
        g.tl[rows + 1] = g.edge_i[0, 0:16]
        g.wl[rows + 1] = g.edge_i[0, 16:32]

    @pl.when(me == nrow - 1)
    def _():
        g.f2[rows + 2 : rows + 4] = jnp.zeros((2, images, cols, C), BF)
        g.tl[rows + 1] = jnp.zeros((16, L), F32)
        g.wl[rows + 1] = jnp.zeros((16, L), F32)


    merge(0, 2, me == 0)
    merge(rows + 2, 2, me == nrow - 1)
    forward([(0, 2), (rows, 2)])
    progress("forward")

    inner = g.d2[1 : rows + 1][:, :, C : 2 * C].reshape(rows * L, C)
    for dy in range(3):
        grad = dot(g.x2[dy + 1 : dy + 1 + rows].reshape(rows * L, 3 * C), inner, TN)
        for dx in range(3):
            store_tap(9 + dy * 3 + dx, grad[dx * C : (dx + 1) * C])
        progress(("conv2a", "conv2b", "conv2")[dy])

    total = sum(
        dot(
            g.d2[2 - dy : 2 - dy + rows].reshape(rows * L, 3 * C)[:, dx * C : (dx + 1) * C],
            g.k2[(dy * 3 + dx) * C : (dy * 3 + dx + 1) * C],
            NT,
        )
        for dy in range(3)
        for dx in range(3)
    )
    g.dm[...] = total.astype(BF).reshape(rows, L, C)
    for q in range(strip):
        pair = total[2 * q * L : (2 * q + 1) * L] + total[(2 * q + 1) * L : (2 * q + 2) * L]
        for half in range(2):
            g.ps[q, half] = pair[:, half * LANES : (half + 1) * LANES]
            value = (
                g.ps[q, half, pl.ds(0, L // 2, stride=2), :]
                + g.ps[q, half, pl.ds(1, L // 2, stride=2), :]
            )
            g.dup_f[:, q * W3 : (q + 1) * W3, half * LANES : (half + 1) * LANES] = value.reshape(
                images, W3, LANES
            )
    g.dup_s[...] = g.dup_f[...].astype(BF)
    dup_sends = []
    for distance in range(1, nrow):
        other = place.in_row(distance)
        dup_sends.append(transfers.send(g.dup_s.at[other], g.dup_r.at[me], (place.img, other)))
    g.dup_r[me] = g.dup_s[me]
    progress("backward")

    dpred2 = jnp.concatenate([g.dpl[1 + f] for f in range(rows)], axis=1)
    g.tin[0:16] += dot(dpred2, g.p2[1 : rows + 1].reshape(rows * L, C))
    hbias_g += jnp.sum(dpred2.astype(F32), axis=1, keepdims=True)
    loss += jnp.sum(sum(g.lossl[1 + f] for f in range(rows)), axis=1, keepdims=True)
    g.tin[20:21, 0:LANES] = jnp.sum(jnp.where(diagonal, hbias_g, 0.0), axis=0, keepdims=True)
    g.tin[20:21, LANES:] = jnp.sum(
        jnp.broadcast_to(loss, (16, LANES)), axis=0, keepdims=True
    )
    g.tin[18:19] = jnp.sum(inner.astype(F32), axis=0, keepdims=True)
    g.tin[21:24] = jnp.zeros((3, C), F32)
    dm = g.dm[...].reshape(rows * L, C)
    store_tap(18, dot(g.f2[2 : rows + 2].reshape(rows * L, C), dm, TN))
    g.tin[16:17] = jnp.sum(dm.astype(F32), axis=0, keepdims=True)
    progress("lat2")

    for copy in dup_sends:
        copy.wait()
    dup = g.dup_r[...].reshape(plan.cells3, C).astype(F32)
    dtop = jnp.concatenate([g.dtop_s[0], g.dtop_s[1]], axis=1) + dup
    dtop_r = dtop.astype(BF)
    lat3_g = dot(g.f3[...], dtop_r, TN)
    store_tap(19, lat3_g[0:TAP])
    store_tap(20, lat3_g[TAP:])
    g.tin[17:18] = jnp.sum(dtop_r.astype(F32), axis=0, keepdims=True)
    small.ready = True
    for copy in late:
        copy.wait()
    progress("lat3")

    while any(job.todo for job in jobs + [small]):
        small.step()
        for job in jobs:
            job.step()
    transfers.close()


def write_kernel(*refs):
    ins, outs, sem = refs[:21], refs[21:42], refs[42]
    copies = []
    for index in range(1, 21):
        src, dst = ins[index], outs[index]
        pairs = [(src, dst)]
        if len(src.shape) == 3:
            pairs = [(src.at[level], dst.at[level]) for level in range(src.shape[0])]
        for pair in pairs:
            copies.append(pltpu.make_async_copy(*pair, sem.at[len(copies)]))
            copies[-1].start()
    outs[0][0] = jnp.max(ins[0][4:5])
    for copy in copies:
        copy.wait()


def body(
    mesh_shape,
    feats2,
    feats3,
    match2,
    target2,
    match3,
    target3,
    positives,
    step_count,
    lat2_w,
    lat2_m,
    lat2_v,
    lat3_w,
    lat3_m,
    lat3_v,
    conv_w,
    conv_m,
    conv_v,
    head_w,
    head_m,
    head_v,
    bias_w,
    bias_m,
    bias_v,
):
    plan = Plan(mesh_shape, feats2.shape, feats3.shape)
    C, L, H3, W3 = plan.width, plan.lanes, plan.high3, plan.cols3
    images, rows, cols, strip, nrow = plan.images, plan.rows, plan.cols, plan.strip, plan.nrow
    head = [x.T for x in (head_w, head_m, head_v)]
    weights = [lat2_w, lat2_m, lat2_v, lat3_w, lat3_m, lat3_v, conv_w, conv_m, conv_v]
    weights += head + [bias_w, bias_m, bias_v]
    args = [
        feats2,
        feats3.reshape(plan.cells3, plan.width3),
        match2,
        target2,
        match3.transpose(0, 1, 3, 2),
        target3.transpose(0, 1, 3, 2),
    ]
    args = [pltpu.with_memory_space_constraint(x, HBM) for x in args]
    held = [pltpu.with_memory_space_constraint(x, HBM) for x in weights]
    hbm, vmem, smem = (pl.BlockSpec(memory_space=space) for space in (HBM, VMEM, SMEM))
    outs = [VMEM((8, LANES), F32)]
    for x in (lat2_w, lat3_w, conv_w, head[0], bias_w):
        outs += [VMEM(x.shape, F32)] * 3 + [VMEM(x.shape, BF)]
    span = (strip + 2) * W3
    dma = pltpu.SemaphoreType.DMA
    remotes = 2 * (nrow - 1) + 6 + plan.tiny_links + len(plan.jobs) * 2 * plan.links
    scratch = [
        VMEM((plan.total, LANES), F32),
        VMEM((plan.total, LANES), BF),
        VMEM((plan.total, LANES), BF),
        VMEM((plan.total, LANES), BF),
        VMEM((plan.total, LANES), BF),
        VMEM((2, plan.total, LANES), BF),
        VMEM((TINY, C), F32),
        VMEM((sum(plan.size.values()), TINY, C), F32),
        VMEM((plan.cells3, plan.width3), BF),
        VMEM((2, plan.cells3 + 16, LANES), F32),
        VMEM((plan.cells3 + 16, C), BF),
        VMEM((nrow, span, C), BF),
        VMEM((W3 + 2, H3, 3 * C), BF),
        VMEM((W3 + 2, H3, 3 * C), BF),
        VMEM((3, 3 * C, C), BF),
        VMEM((12, W3, H3), F32),
        VMEM((3, W3, H3), jnp.int32),
        VMEM((2, 16 * W3, LANES), F32),
        VMEM((2, plan.cells3, LANES), F32),
        VMEM((rows + 4, images, cols, C), BF),
        VMEM((strip + 2, images, cols, C), F32),
        VMEM((rows + 4, L, 3 * C), BF),
        VMEM((rows + 2, L, 3 * C), BF),
        VMEM((rows + 2, L, C), BF),
        VMEM((9 * C, C), BF),
        VMEM(target2.shape, F32),
        VMEM(match2.shape, jnp.int32),
        VMEM((L // LANES, 16 * rows, LANES), F32),
        VMEM((L // LANES, 16 * rows, LANES), F32),
        VMEM((2, 32, L), F32),
        VMEM((2, 32, L), F32),
        VMEM((rows + 2, 16, L), F32),
        VMEM((rows + 2, 16, L), F32),
        VMEM((rows + 2, 16, L), BF),
        VMEM((rows + 2, 16, L), F32),
        VMEM((strip, 2, L, LANES), F32),
        VMEM((images, strip * W3, C), F32),
        VMEM((images, strip * W3, C), BF),
        VMEM((nrow, strip * W3, C), BF),
        VMEM((rows, L, C), BF),
        VMEM((16, 3 * LANES), F32),
        VMEM((16, C), BF),
        VMEM((C, C), BF),
        dma((48,)),
        dma((remotes,)),
        dma((remotes,)),
    ]
    results = pl.pallas_call(
        functools.partial(main_kernel, plan),
        out_shape=outs,
        in_specs=[hbm] * 6 + [smem] * 2 + [hbm] * len(held),
        out_specs=[vmem] * len(outs),
        scratch_shapes=scratch,
        compiler_params=pltpu.CompilerParams(
            collective_id=0, has_side_effects=True, vmem_limit_bytes=40 << 20
        ),
        name="gradients",
    )(*args, positives.reshape(1), step_count.reshape(1), *held)
    kept = [pltpu.with_memory_space_constraint(x, VMEM) for x in results]

    shapes = [jax.ShapeDtypeStruct((1,), F32)]
    shapes += [jax.ShapeDtypeStruct(x.shape, x.dtype) for x in kept[1:]]
    new = pl.pallas_call(
        write_kernel,
        out_shape=shapes,
        in_specs=[vmem] * len(kept),
        out_specs=[smem] + [hbm] * 20,
        scratch_shapes=[dma((24,))],
        compiler_params=pltpu.CompilerParams(vmem_limit_bytes=1 << 20),
        name="results",
    )(*kept)
    outs = [new[0].reshape(())] + list(new[1:])
    for index in range(13, 17):
        outs[index] = outs[index].T
    return tuple(outs)


def solution(mesh):
    split = (
        P("img", "row", None, None),
        P(("img", "row"), None, None, None),
        P("img", None, "row", None),
        P("img", None, "row", None),
        P(("img", "row"), None, None, None),
        P(("img", "row"), None, None, None),
    )
    return jax.shard_map(
        functools.partial(body, dict(mesh.shape)),
        mesh=mesh,
        in_specs=split + (P(),) * 17,
        out_specs=(P(),) * 21,
        check_vma=False,
    )
```
